32 devices in a mesh: groups: 2 (over y), mom: 4 (over z), tm: 4 (over x, core).
Axes of the slice: x: 2, y: 2, z: 4, core: 2. Of those that a mesh axis runs over, the one named last changes fastest.
Arguments:
- panel_start: float32 [256, 4, 64, 512], P('mom', 'groups', None, 'tm'), parts along dimension 1, may hold values from -6 to 6
- block_guess: float32 [256, 4, 64, 128], P('mom', 'groups', 'tm'), parts along dimension 1, may hold values from -6 to 6
- coupling: float32 [2], P('groups'), parts along dimension 0, may hold values from 0.3 to 0.6
- slab_owner: int32 [8], P('groups'), parts along dimension 0, may hold values from 0 to 3, each once
- expiring: int32 [2], P('groups'), parts along dimension 0, may hold values from 0 to 3
- ordering: int32 [256], replicated, may hold values from 0 to 255, each once
Outputs:
- history_out: float32 [256, 4, 64, 512], P('mom', 'groups', None, 'tm'), parts along dimension 1
The draws below stay inside these ranges and needn't reach their ends.
There are 2 independent parts, one for each index of `groups`. The reference program is written for one: setup_inputs(seed, part) draws one part's arguments, and reference() takes and returns one part's arrays. A program takes and returns all parts, laid end to end along the dimension named above; an argument that names none is the same for every part. Nothing has to cross between parts.
Inputs may be any that keep to these rules, and one draw needn't show every extreme that they name: `slab_owner`: entry s is the column block that holds history slab s; each block once. `ordering`: entry j is qx * 16 + qy for the momentum of stored row j; each momentum once.
All inputs are finite; a program needn't handle non-finite values.
Results may differ from the reference program's by a relative error of at most 0.0001.
Values sent between devices are 32-bit elements; how exact they have to be, the bound alone decides.
No kernel may reach another device: no remote copies, remote signals or barrier semaphores. Data moves between devices by JAX's collectives and lax.ppermute only.
A program may use at most 128 MiB of HBM per device.

```python
import math
import jax
import jax.numpy as jnp
from jax import lax

LSIDE = 16
K = 256
SPIN = 2
PANEL = 64
PASSES = 2
HIST = 256
N_TM = 4


def block_levels(key, shape, cuts, smallest, largest):
    gain, own = 1.0, jax.random.fold_in(key, 6)
    for axis_at, shards_of in cuts:
        heights = jnp.exp(jax.random.uniform(jax.random.fold_in(own, axis_at), (shards_of,), jnp.float32, smallest / len(cuts), largest / len(cuts)))
        gain = gain * jnp.repeat(heights, shape[axis_at] // shards_of).reshape([-1 if axis == axis_at else 1 for axis in range(len(shape))])
    return gain


def normal_values(stream_key, extent, width, most, cuts=(), kind=jnp.bfloat16):
    values = jax.random.normal(stream_key, extent, jnp.float32) * width
    if len(cuts) > 0:
        values = block_levels(stream_key, extent, cuts, -0.22, 0.18) * values
    return jnp.clip(values, min=-most, max=most).astype(kind)


def setup_inputs(seed: int = 0, part: int = 0) -> dict:
    keys = jax.random.split(jax.random.key(seed), 7)
    part_keys = jax.random.split(jax.random.fold_in(keys[6], part), 7)
    panel_start = normal_values(part_keys[0], (K, SPIN, PANEL, 2 * HIST), 1.0, 6.0, ((0, 4), (3, 4)), jnp.float32)
    block_guess = normal_values(part_keys[1], (K, SPIN, PANEL, 2 * PANEL), 1.0, 6.0, ((0, 4), (2, 4)), jnp.float32)
    coupling = jnp.clip(jnp.exp(jax.random.uniform(part_keys[2], (1,), jnp.float32, math.log(0.3), math.log(0.6))), 0.3, 0.6)
    slab_owner = jax.random.permutation(part_keys[3], N_TM).astype(jnp.int32)
    expiring = jax.random.randint(part_keys[4], (1,), 0, N_TM).astype(jnp.int32)
    ordering = jax.random.permutation(keys[5], K).astype(jnp.int32)
    return dict(panel_start=panel_start, block_guess=block_guess, coupling=coupling, slab_owner=slab_owner, expiring=expiring, ordering=ordering)


def product(left, right):
    return jnp.dot(left, right, precision=lax.Precision.HIGHEST, preferred_element_type=jnp.float32)

def contract(pattern, left, right):
    return jnp.einsum(pattern, left, right, precision=lax.Precision.HIGHEST, preferred_element_type=jnp.float32)

def tables(ordering):
    site_index = jnp.arange(K, dtype=jnp.int32)
    site_x = site_index // LSIDE
    site_y = site_index % LSIDE
    mom_x = ordering // LSIDE
    mom_y = ordering % LSIDE
    phases = (site_x[:, None] * mom_x[None, :] + site_y[:, None] * mom_y[None, :]) % LSIDE
    angles = phases.astype(jnp.float32) * (2.0 * math.pi / LSIDE)
    mirror = (-site_x % LSIDE * LSIDE + -site_y % LSIDE).astype(jnp.int32)
    return (jnp.cos(angles) / LSIDE, jnp.sin(angles) / LSIDE, mirror)

def site_sigma(mom_re, mom_im, cos_table, sin_table, mirror, strength):
    layout = mom_re.shape
    flat_re = mom_re.reshape(K, -1)
    flat_im = mom_im.reshape(K, -1)
    site_re = (product(cos_table, flat_re) - product(sin_table, flat_im)).reshape(layout)
    site_im = (product(cos_table, flat_im) + product(sin_table, flat_re)).reshape(layout)
    other_re = site_re[:, ::-1]
    other_im = site_im[:, ::-1]
    pair_re = site_re * other_re - site_im * other_im
    pair_im = site_re * other_im + site_im * other_re
    back_re = jnp.take(other_re, mirror, axis=0)
    back_im = jnp.take(other_im, mirror, axis=0)
    sig_re = (-strength * (pair_re * back_re + pair_im * back_im)).reshape(K, -1)
    sig_im = (-strength * (pair_im * back_re - pair_re * back_im)).reshape(K, -1)
    out_re = product(cos_table.T, sig_re) + product(sin_table.T, sig_im)
    out_im = product(cos_table.T, sig_im) - product(sin_table.T, sig_re)
    return (out_re.reshape(layout), out_im.reshape(layout))

def reference(panel_start, block_guess, coupling, slab_owner, expiring, ordering):
    cos_table, sin_table, mirror = tables(ordering)
    blocks = jnp.arange(N_TM, dtype=jnp.int32)
    slab_of = lax.optimization_barrier(jnp.sum(blocks[None, :] * (slab_owner[None, :] == blocks[:, None]).astype(jnp.int32), axis=1))
    position = (slab_of - expiring[0]) % N_TM
    times = position[:, None] * PANEL + jnp.arange(PANEL, dtype=jnp.int32)[None, :]
    window = N_TM * PANEL
    weights = jnp.exp(-1.5 * (window - 1 - times).astype(jnp.float32) / window) / math.sqrt(window)
    strength = coupling[0] * coupling[0]
    step_scale = 1.0 / math.sqrt(PANEL)
    split = panel_start.reshape(K, SPIN, PANEL, N_TM, 2, PANEL)
    start_re = split[:, :, :, :, 0, :]
    start_im = split[:, :, :, :, 1, :]
    current_re, current_im = (start_re, start_im)
    conv_re = jnp.zeros((K, SPIN, PANEL, PANEL), jnp.float32)
    conv_im = jnp.zeros((K, SPIN, PANEL, PANEL), jnp.float32)
    for sweep in range(PASSES):
        sig_re, sig_im = site_sigma(current_re, current_im, cos_table, sin_table, mirror, strength)
        sig_re = sig_re * weights
        sig_im = sig_im * weights
        conv_re = -(contract('ksadu,ksbdu->ksab', sig_re, current_re) + contract('ksadu,ksbdu->ksab', sig_im, current_im))
        conv_im = -(contract('ksadu,ksbdu->ksab', sig_im, current_re) - contract('ksadu,ksbdu->ksab', sig_re, current_im))
        next_re = start_re + step_scale * (contract('ksab,ksbdu->ksadu', conv_re, current_re) - contract('ksab,ksbdu->ksadu', conv_im, current_im))
        next_im = start_im + step_scale * (contract('ksab,ksbdu->ksadu', conv_re, current_im) + contract('ksab,ksbdu->ksadu', conv_im, current_re))
        current_re, current_im = (next_re, next_im)
    guess_re = block_guess[..., :PANEL]
    guess_im = block_guess[..., PANEL:]
    block_re = guess_re + step_scale * (contract('ksab,ksbc->ksac', guess_re, conv_re) - contract('ksab,ksbc->ksac', guess_im, conv_im))
    block_im = guess_im + step_scale * (contract('ksab,ksbc->ksac', guess_re, conv_im) + contract('ksab,ksbc->ksac', guess_im, conv_re))
    history = jnp.stack([current_re, current_im], axis=4)
    block = jnp.stack([block_re, block_im], axis=3)[:, :, :, None]
    owner_expiring = jnp.sum(slab_owner * (blocks == expiring[0]).astype(jnp.int32))
    chosen = (blocks == owner_expiring)[:, None, None]
    merged = jnp.where(chosen, block, history)
    return merged.reshape(K, SPIN, PANEL, 2 * window)
```

```python
import functools
import math

import jax
import jax.numpy as jnp
from jax import lax
from jax.experimental import pallas as pl
from jax.experimental.pallas import tpu as pltpu
from jax.sharding import PartitionSpec as P

LSIDE = 16
K = 256
PASSES = 2
CHUNKS = 2
ROWS = 8
LANES = 128
KBLOCK = 8
VMEM_LIMIT = 48 * 2**20
f32, bf16 = jnp.float32, jnp.bfloat16


def window_weights(slab_owner, expiring, own_index, slab_count, panel):
    blocks = jnp.arange(slab_count, dtype=jnp.int32)
    slab_mine = jnp.sum(blocks * (slab_owner == own_index).astype(jnp.int32))
    position = (slab_mine - expiring[0]) % slab_count
    window = slab_count * panel
    times = position * panel + jnp.arange(panel, dtype=jnp.int32)
    weights = jnp.exp(-1.5 * (window - 1 - times).astype(f32) / window) / math.sqrt(window)
    owner_expiring = jnp.sum(slab_owner * (blocks == expiring[0]).astype(jnp.int32))
    return jnp.concatenate([weights, weights]), own_index == owner_expiring


def phases(ordering):
    site = jnp.arange(K, dtype=jnp.int32)
    turn = (
        (site // LSIDE)[:, None] * (ordering // LSIDE)[None, :]
        + (site % LSIDE)[:, None] * (ordering % LSIDE)[None, :]
    ) % LSIDE
    angles = turn.astype(f32) * (2.0 * math.pi / LSIDE)
    return jnp.cos(angles) / LSIDE, jnp.sin(angles) / LSIDE


def product(left, right):
    return jnp.dot(left, right, precision=lax.Precision.HIGHEST, preferred_element_type=f32)


def contract(pattern, left, right):
    return jnp.einsum(
        pattern, left, right, precision=lax.Precision.HIGHEST, preferred_element_type=f32
    )


def rotated(joined):
    half = joined.shape[-1] // 2
    return jnp.concatenate([-joined[..., half:], joined[..., :half]], axis=-1)


def plain_sigma(joined, cos_table, sin_table, strength):
    layout, half = joined.shape, joined.shape[-1] // 2
    flat = joined.reshape(K, -1)
    with_cos = product(cos_table, flat).reshape(layout)
    with_sin = product(sin_table, flat).reshape(layout)
    c_re, c_im = with_cos[..., :half], with_cos[..., half:]
    s_re, s_im = with_sin[..., :half], with_sin[..., half:]
    site_re, site_im = c_re - s_im, c_im + s_re
    back_re, back_im = (c_re + s_im)[:, ::-1], (c_im - s_re)[:, ::-1]
    other_re, other_im = site_re[:, ::-1], site_im[:, ::-1]
    pair_re = site_re * other_re - site_im * other_im
    pair_im = site_re * other_im + site_im * other_re
    sig_re = -strength * (pair_re * back_re + pair_im * back_im)
    sig_im = -strength * (pair_im * back_re - pair_re * back_im)
    sig = jnp.concatenate([sig_re, sig_im], axis=-1).reshape(K, -1)
    back_cos = product(cos_table.T, sig).reshape(layout)
    back_sin = product(sin_table.T, sig).reshape(layout)
    out_re = back_cos[..., :half] + back_sin[..., half:]
    out_im = back_cos[..., half:] - back_sin[..., :half]
    return jnp.concatenate([out_re, out_im], axis=-1)


def plain_body(panel_start, block_guess, coupling, slab_owner, expiring, ordering):
    panel = panel_start.shape[2]
    weights, chosen = window_weights(
        slab_owner, expiring, lax.axis_index("tm"), lax.axis_size("tm"), panel
    )
    cos_table, sin_table = phases(ordering)
    strength = coupling[0] * coupling[0]
    step_scale = 1.0 / math.sqrt(panel)
    guess = lax.all_gather(block_guess, "tm", axis=2, tiled=True)
    current = panel_start
    for _ in range(PASSES):
        exchanged = lax.all_to_all(current, "mom", split_axis=2, concat_axis=0, tiled=True)
        sigma = plain_sigma(exchanged, cos_table, sin_table, strength)
        returned = lax.all_to_all(sigma, "mom", split_axis=0, concat_axis=2, tiled=True)
        stacked = jnp.concatenate([current, rotated(current)], axis=2)
        conv = lax.psum(-contract("ksau,ksbu->ksab", returned * weights, stacked), "tm")
        current = panel_start + step_scale * contract("ksab,ksbu->ksau", conv, stacked)
    stacked = jnp.concatenate([conv, rotated(conv)], axis=2)
    block = guess + step_scale * contract("ksab,ksbc->ksac", guess, stacked)
    return jnp.where(chosen, block, current)


def split(x):
    high = x.astype(bf16)
    return high, (x - high.astype(f32)).astype(bf16)


def dot(left, right, transposed=False):
    dims = (((1,), (1 if transposed else 0,)), ((), ()))
    return lax.dot_general(left, right, dims, preferred_element_type=f32)


def dot3(left, right, transposed=False):
    (lh, ll), (rh, rl) = left, right
    rows = lh.shape[0]
    both = dot(jnp.concatenate([lh, ll], axis=0), rh, transposed)
    return both[:rows] + (both[rows:] + dot(lh, rl, transposed))


def first_half(shape):
    return lax.broadcasted_iota(jnp.int32, shape, 1) < LANES // 2


def swap(x):
    return pltpu.roll(x, LANES // 2, 1)


def stack_rotated(g):
    other = swap(g)
    return jnp.concatenate([g, jnp.where(first_half(g.shape), -other, other)], axis=0)


def site_kernel(count, rows, strength_ref, weight_ref, fh_ref, fl_ref, bh_ref, bl_ref, *refs):
    x_refs, y_refs = refs[:count], refs[count:]
    span = K // count
    stride = 2 * rows
    left = first_half((K, LANES))
    weight = weight_ref[...]
    scale = -strength_ref[0]

    def take(spin, row):
        return jnp.concatenate(
            [x[pl.ds(spin * rows + row, span, stride=stride), :] for x in x_refs], axis=0
        )

    @pl.loop(0, rows // 2)
    def _(pair):
        site = []
        for spin in range(2):
            a, b = take(spin, 2 * pair), take(spin, 2 * pair + 1)
            re = jnp.where(left, a, swap(b))
            im = jnp.where(left, swap(a), b)
            joined = split(jnp.concatenate([re, im], axis=1))
            out = dot3((fh_ref[...], fl_ref[...]), joined)
            c_re, c_im = out[:K, :LANES], out[:K, LANES:]
            s_re, s_im = out[K:, :LANES], out[K:, LANES:]
            site.append((c_re - s_im, c_im + s_re, c_re + s_im, c_im - s_re))
        (r0, i0, *_), (r1, i1, *_) = site
        pair_re = scale * (r0 * r1 - i0 * i1)
        pair_im = scale * (r0 * i1 + i0 * r1)
        for spin in range(2):
            _, _, m_re, m_im = site[1 - spin]
            sig_re = pair_re * m_re + pair_im * m_im
            sig_im = pair_im * m_re - pair_re * m_im
            joined = split(jnp.concatenate([sig_re, sig_im], axis=1))
            out = dot3((bh_ref[...], bl_ref[...]), joined)
            re = (out[:K, :LANES] + out[K:, LANES:]) * weight
            im = (out[:K, LANES:] - out[K:, :LANES]) * weight
            a = jnp.where(left, re, swap(im))
            b = jnp.where(left, swap(re), im)
            for d, y in enumerate(y_refs):
                place = pl.ds(spin * rows + 2 * pair, span, stride=stride)
                y[place, :] = a[d * span : (d + 1) * span]
                place = pl.ds(spin * rows + 2 * pair + 1, span, stride=stride)
                y[place, :] = b[d * span : (d + 1) * span]


def site_sigma(strength, weights, tables, blocks):
    shape = blocks[0].shape
    rows, count = shape[2], len(blocks)
    flat = [x.reshape(-1, LANES) for x in blocks]
    vmem = pl.BlockSpec(memory_space=pltpu.VMEM)
    outs = pl.pallas_call(
        functools.partial(site_kernel, count, rows),
        out_shape=[jax.ShapeDtypeStruct(x.shape, f32) for x in flat],
        in_specs=[pl.BlockSpec(memory_space=pltpu.SMEM)] + [vmem] * (5 + count),
        out_specs=[vmem] * count,
        compiler_params=pltpu.CompilerParams(vmem_limit_bytes=VMEM_LIMIT),
        cost_estimate=pl.CostEstimate(
            flops=2 * 2 * 3 * 2 * K * K * 2 * rows * LANES, bytes_accessed=8 * K * 2 * rows * LANES, transcendentals=0
        ),
        name="site_sigma",
    )(strength, weights, *tables, *flat)
    return [y.reshape(shape) for y in outs]


def place_of(info_ref, d, rows):
    return pl.ds(pl.multiple_of((info_ref[1] ^ d) * rows, rows), rows)


def conv_kernel(count, parts, info_ref, *refs):
    s_refs, g_refs, c_ref = refs[:count], refs[count : count + parts], refs[-1]
    rows = s_refs[0].shape[2]
    for k in range(c_ref.shape[0]):
        for spin in range(2):
            s = split(jnp.concatenate([x[k, spin] for x in s_refs], axis=0))
            g = jnp.concatenate([x[k, spin] for x in g_refs], axis=0)
            out = -dot3(s, split(stack_rotated(g)), transposed=True)
            for d in range(count):
                c_ref[k, spin, place_of(info_ref, d, rows), :] = out[d * rows : (d + 1) * rows]


def conv_rows(info, blocks, g_parts, kcount):
    count, rows = len(blocks), blocks[0].shape[2]
    moved = lambda i, info: (info[0] + i, 0, 0, 0)
    return pl.pallas_call(
        functools.partial(conv_kernel, count, len(g_parts)),
        out_shape=jax.ShapeDtypeStruct((kcount, 2, count * rows, LANES), f32),
        grid_spec=pltpu.PrefetchScalarGridSpec(
            num_scalar_prefetch=1,
            grid=(kcount // KBLOCK,),
            in_specs=[pl.BlockSpec((KBLOCK, *x.shape[1:]), moved) for x in (*blocks, *g_parts)],
            out_specs=pl.BlockSpec((KBLOCK, 2, count * rows, LANES), lambda i, info: (i, 0, 0, 0)),
        ),
        compiler_params=pltpu.CompilerParams(vmem_limit_bytes=VMEM_LIMIT),
        cost_estimate=pl.CostEstimate(
            flops=kcount * 2 * 3 * 2 * count * rows * LANES * LANES,
            bytes_accessed=4 * kcount * 2 * LANES * (2 * count * rows + 64),
            transcendentals=0,
        ),
        name="conv_rows",
    )(info, *blocks, *g_parts)


def chosen_half(info_ref, mine_ref, other_ref, k, spin):
    steps = pl.num_programs(0) // 2
    own = (pl.program_id(0) // steps) == info_ref[2]
    return jnp.where(own, mine_ref[k, spin], other_ref[k, spin])


def update_kernel(count, chunk, step_scale, info_ref, mine_ref, other_ref, g_ref, now_ref, *blk_refs):
    rows = blk_refs[0].shape[2]
    total = count * rows
    for k in range(now_ref.shape[0]):
        for spin in range(2):
            c = split(chosen_half(info_ref, mine_ref, other_ref, k, spin))
            g = g_ref[k, spin]
            moved = dot3(c, split(stack_rotated(g)))
            now_ref[k, spin] = g_ref[k, spin, pl.ds(chunk * total, total), :] + step_scale * moved
            for d, blk in enumerate(blk_refs):
                blk[k, spin] = now_ref[k, spin, place_of(info_ref, d, rows), :]


def update_rows(info, mine, other, panel_start, chunk, count, step_scale):
    momenta, spins, panel, _ = panel_start.shape
    total = mine.shape[2]
    rows = total // count
    grid = momenta // KBLOCK
    halved = lambda i, info: (i % (grid // 2), 0, 0, 0)
    plain = lambda i, info: (i, 0, 0, 0)
    return pl.pallas_call(
        functools.partial(update_kernel, count, chunk, step_scale),
        out_shape=[jax.ShapeDtypeStruct((momenta, spins, total, LANES), f32)]
        + [jax.ShapeDtypeStruct((momenta, spins, rows, LANES), f32)] * count,
        grid_spec=pltpu.PrefetchScalarGridSpec(
            num_scalar_prefetch=1,
            grid=(grid,),
            in_specs=[pl.BlockSpec((KBLOCK, spins, total, LANES), halved)] * 2
            + [pl.BlockSpec((KBLOCK, spins, panel, LANES), plain)],
            out_specs=[pl.BlockSpec((KBLOCK, spins, total, LANES), plain)]
            + [pl.BlockSpec((KBLOCK, spins, rows, LANES), plain)] * count,
        ),
        compiler_params=pltpu.CompilerParams(vmem_limit_bytes=VMEM_LIMIT),
        cost_estimate=pl.CostEstimate(
            flops=momenta * spins * 3 * 2 * total * LANES * LANES,
            bytes_accessed=4 * momenta * spins * LANES * (4 * total + panel),
            transcendentals=0,
        ),
        name="update_rows",
    )(info, mine, other, panel_start)


def final_kernel(chunk, parts, step_scale, info_ref, mine_ref, other_ref, start_ref, *refs):
    g_refs, guess_ref, prev_ref, out_ref = refs[:parts], refs[parts], refs[parts + 1], refs[-1]
    total = mine_ref.shape[2]
    panel = start_ref.shape[2]
    here = pl.ds(chunk * total, total)

    @pl.when(info_ref[3] == 0)
    def _():
        for k in range(out_ref.shape[0]):
            for spin in range(2):
                c = split(chosen_half(info_ref, mine_ref, other_ref, k, spin))
                g = jnp.concatenate([x[k, spin] for x in g_refs], axis=0)
                moved = dot3(c, split(stack_rotated(g)))
                if chunk > 0:
                    out_ref[k, spin, pl.ds(0, chunk * total), :] = prev_ref[k, spin, pl.ds(0, chunk * total), :]
                out_ref[k, spin, here, :] = start_ref[k, spin, here, :] + step_scale * moved
                if (chunk + 1) * total < panel:
                    rest = pl.ds((chunk + 1) * total, panel - (chunk + 1) * total)
                    out_ref[k, spin, rest, :] = start_ref[k, spin, rest, :]

    @pl.when(info_ref[3] == 1)
    def _():
        for k in range(out_ref.shape[0]):
            for spin in range(2):
                c = chosen_half(info_ref, mine_ref, other_ref, k, spin)
                d = guess_ref[k, spin]
                at = chunk * total
                d_re = d[:, at : at + total]
                d_im = d[:, panel + at : panel + at + total]
                sides = split(jnp.concatenate([d_re, d_im], axis=1))
                moved = dot3(sides, split(stack_rotated(c)))
                so_far = d if chunk == 0 else prev_ref[k, spin]
                out_ref[k, spin] = so_far + step_scale * moved


def final_rows(info, mine, other, panel_start, g_parts, guess, previous, chunk, step_scale):
    momenta, spins, panel, _ = panel_start.shape
    total = mine.shape[2]
    grid = momenta // KBLOCK
    halved = lambda i, info: (i % (grid // 2), 0, 0, 0)
    plain = lambda i, info: (i, 0, 0, 0)
    whole = pl.BlockSpec((KBLOCK, spins, panel, LANES), plain)
    return pl.pallas_call(
        functools.partial(final_kernel, chunk, len(g_parts), step_scale),
        out_shape=jax.ShapeDtypeStruct(panel_start.shape, f32),
        grid_spec=pltpu.PrefetchScalarGridSpec(
            num_scalar_prefetch=1,
            grid=(grid,),
            in_specs=[pl.BlockSpec((KBLOCK, spins, total, LANES), halved)] * 2
            + [whole]
            + [pl.BlockSpec((KBLOCK, *g.shape[1:]), plain) for g in g_parts]
            + [whole, whole],
            out_specs=whole,
        ),
        compiler_params=pltpu.CompilerParams(vmem_limit_bytes=VMEM_LIMIT),
        cost_estimate=pl.CostEstimate(
            flops=momenta * spins * 3 * 2 * total * LANES * LANES,
            bytes_accessed=4 * momenta * spins * LANES * 5 * panel,
            transcendentals=0,
        ),
        name="final_rows",
    )(info, mine, other, panel_start, *g_parts, guess, previous)


def pairs(size, d):
    return [(i, i ^ d) for i in range(size)]


def exchange(blocks):
    size = len(blocks)
    return [blocks[0]] + [lax.ppermute(blocks[d], "mom", pairs(size, d)) for d in range(1, size)]


def table_parts(ordering, my_mom, count):
    span = K // count
    local = jnp.concatenate(
        [lax.dynamic_slice(ordering, ((my_mom ^ d) * span,), (span,)) for d in range(count)]
    )
    cos_table, sin_table = phases(local)
    out = []
    for table in (
        jnp.concatenate([cos_table, sin_table], axis=0),
        jnp.concatenate([cos_table.T, sin_table.T], axis=0),
    ):
        high = lax.reduce_precision(table, exponent_bits=8, mantissa_bits=7)
        out += [high.astype(bf16), (table - high).astype(bf16)]
    return out


def body(panel_start, block_guess, coupling, slab_owner, expiring, ordering):
    momenta, spins, panel, _ = panel_start.shape
    count, slabs = lax.axis_size("mom"), lax.axis_size("tm")
    my_mom, my_tm = lax.axis_index("mom"), lax.axis_index("tm")
    weights, chosen = window_weights(slab_owner, expiring, my_tm, slabs, panel)
    weights = weights.reshape(1, LANES)
    strength = coupling * coupling
    step_scale = 1.0 / math.sqrt(panel)
    total = panel // CHUNKS
    rows = total // count
    half = momenta // 2
    core = my_tm % 2
    flag = chosen.astype(jnp.int32)

    def info(k_half):
        return jnp.stack([k_half * (half // KBLOCK), my_mom, core, flag]).astype(jnp.int32)

    def share(chunk, d):
        at = chunk * total + (my_mom ^ d) * rows
        return lax.dynamic_slice(panel_start, (0, 0, at, 0), (momenta, spins, rows, LANES))

    def summed(give, keep):
        mine = keep + lax.ppermute(give, "tm", pairs(slabs, 1))
        bit = 2
        while bit < slabs:
            mine = mine + lax.ppermute(mine, "tm", pairs(slabs, bit))
            bit *= 2
        return mine, lax.ppermute(mine, "tm", pairs(slabs, 1))

    sent = [[share(c, d) for d in range(count)] for c in range(CHUNKS)]
    tables = table_parts(ordering, my_mom, count)
    g_parts = [panel_start]
    plain_info = info(core)
    for sweep in range(PASSES):
        arrived = [exchange(blocks) for blocks in sent]
        sigma = [exchange(site_sigma(strength, weights, tables, blocks)) for blocks in arrived]
        convs = []
        for chunk in range(CHUNKS):
            give = conv_rows(info(1 - core), sigma[chunk], g_parts, half)
            keep = conv_rows(info(core), sigma[chunk], g_parts, half)
            convs.append(summed(give, keep))
        if sweep < PASSES - 1:
            news = [
                update_rows(plain_info, *convs[c], panel_start, c, count, step_scale)
                for c in range(CHUNKS)
            ]
            g_parts = [n[0] for n in news]
            sent = [list(n[1:]) for n in news]
    guess = lax.all_gather(block_guess, "tm", axis=2, tiled=True)
    out = panel_start
    for chunk in range(CHUNKS):
        out = final_rows(plain_info, *convs[chunk], panel_start, g_parts, guess, out, chunk, step_scale)
    return out


def fits(mesh):
    def tiled(panel_start, *_):
        momenta, spins, panel, width = panel_start.shape
        count, slabs = mesh.shape["mom"], mesh.shape["tm"]
        powers = all(n & (n - 1) == 0 for n in (count, slabs))
        local = momenta // count
        return (
            powers
            and slabs > 1
            and spins == 2 * mesh.shape["groups"]
            and width == LANES * slabs
            and 2 * panel == LANES
            and panel == CHUNKS * count * ROWS
            and local % (2 * KBLOCK) == 0
            and PASSES == 2
        )

    return tiled


def solution(mesh):
    def mapped(inner):
        return jax.shard_map(
            inner,
            mesh=mesh,
            in_specs=(
                P("mom", "groups", None, "tm"),
                P("mom", "groups", "tm", None),
                P("groups"),
                P("groups"),
                P("groups"),
                P(),
            ),
            out_specs=P("mom", "groups", None, "tm"),
            check_vma=False,
        )

    def chosen(*args):
        return mapped(body if fits(mesh)(*args) else plain_body)(*args)

    return chosen
```

```python
import functools
import math

import jax
import jax.numpy as jnp
from jax import lax
from jax.experimental import pallas as pl
from jax.experimental.pallas import tpu as pltpu
from jax.sharding import PartitionSpec as P

LSIDE = 16
K = 256
PASSES = 2
CHUNKS = 2
ROWS = 8
LANES = 128
KBLOCK = 8
VMEM_LIMIT = 48 * 2**20
f32, bf16 = jnp.float32, jnp.bfloat16
SMALL = pl.CostEstimate(flops=1, bytes_accessed=1, transcendentals=0)


def window_weights(slab_owner, expiring, own_index, slab_count, panel):
    blocks = jnp.arange(slab_count, dtype=jnp.int32)
    slab_mine = jnp.sum(blocks * (slab_owner == own_index).astype(jnp.int32))
    position = (slab_mine - expiring[0]) % slab_count
    window = slab_count * panel
    times = position * panel + jnp.arange(panel, dtype=jnp.int32)
    weights = jnp.exp(-1.5 * (window - 1 - times).astype(f32) / window) / math.sqrt(window)
    owner_expiring = jnp.sum(slab_owner * (blocks == expiring[0]).astype(jnp.int32))
    return jnp.concatenate([weights, weights]), own_index == owner_expiring


def phases(ordering):
    site = jnp.arange(K, dtype=jnp.int32)
    turn = (
        (site // LSIDE)[:, None] * (ordering // LSIDE)[None, :]
        + (site % LSIDE)[:, None] * (ordering % LSIDE)[None, :]
    ) % LSIDE
    angles = turn.astype(f32) * (2.0 * math.pi / LSIDE)
    return jnp.cos(angles) / LSIDE, jnp.sin(angles) / LSIDE


def product(left, right):
    return jnp.dot(left, right, precision=lax.Precision.HIGHEST, preferred_element_type=f32)


def contract(pattern, left, right):
    return jnp.einsum(
        pattern, left, right, precision=lax.Precision.HIGHEST, preferred_element_type=f32
    )


def rotated(joined):
    half = joined.shape[-1] // 2
    return jnp.concatenate([-joined[..., half:], joined[..., :half]], axis=-1)


def plain_sigma(joined, cos_table, sin_table, strength):
    layout, half = joined.shape, joined.shape[-1] // 2
    flat = joined.reshape(K, -1)
    with_cos = product(cos_table, flat).reshape(layout)
    with_sin = product(sin_table, flat).reshape(layout)
    c_re, c_im = with_cos[..., :half], with_cos[..., half:]
    s_re, s_im = with_sin[..., :half], with_sin[..., half:]
    site_re, site_im = c_re - s_im, c_im + s_re
    back_re, back_im = (c_re + s_im)[:, ::-1], (c_im - s_re)[:, ::-1]
    other_re, other_im = site_re[:, ::-1], site_im[:, ::-1]
    pair_re = site_re * other_re - site_im * other_im
    pair_im = site_re * other_im + site_im * other_re
    sig_re = -strength * (pair_re * back_re + pair_im * back_im)
    sig_im = -strength * (pair_im * back_re - pair_re * back_im)
    sig = jnp.concatenate([sig_re, sig_im], axis=-1).reshape(K, -1)
    back_cos = product(cos_table.T, sig).reshape(layout)
    back_sin = product(sin_table.T, sig).reshape(layout)
    out_re = back_cos[..., :half] + back_sin[..., half:]
    out_im = back_cos[..., half:] - back_sin[..., :half]
    return jnp.concatenate([out_re, out_im], axis=-1)


def plain_body(panel_start, block_guess, coupling, slab_owner, expiring, ordering):
    panel = panel_start.shape[2]
    weights, chosen = window_weights(
        slab_owner, expiring, lax.axis_index("tm"), lax.axis_size("tm"), panel
    )
    cos_table, sin_table = phases(ordering)
    strength = coupling[0] * coupling[0]
    step_scale = 1.0 / math.sqrt(panel)
    guess = lax.all_gather(block_guess, "tm", axis=2, tiled=True)
    current = panel_start
    for _ in range(PASSES):
        exchanged = lax.all_to_all(current, "mom", split_axis=2, concat_axis=0, tiled=True)
        sigma = plain_sigma(exchanged, cos_table, sin_table, strength)
        returned = lax.all_to_all(sigma, "mom", split_axis=0, concat_axis=2, tiled=True)
        stacked = jnp.concatenate([current, rotated(current)], axis=2)
        conv = lax.psum(-contract("ksau,ksbu->ksab", returned * weights, stacked), "tm")
        current = panel_start + step_scale * contract("ksab,ksbu->ksau", conv, stacked)
    stacked = jnp.concatenate([conv, rotated(conv)], axis=2)
    block = guess + step_scale * contract("ksab,ksbc->ksac", guess, stacked)
    return jnp.where(chosen, block, current)


def split(x):
    high = x.astype(bf16)
    return high, (x - high.astype(f32)).astype(bf16)


def dot(left, right, transposed=False):
    dims = (((1,), (1 if transposed else 0,)), ((), ()))
    return lax.dot_general(left, right, dims, preferred_element_type=f32)


def dot3(left, right, transposed=False):
    (lh, ll), (rh, rl) = left, right
    rows = lh.shape[0]
    both = dot(jnp.concatenate([lh, ll], axis=0), rh, transposed)
    return both[:rows] + (both[rows:] + dot(lh, rl, transposed))


def first_half(shape):
    return lax.broadcasted_iota(jnp.int32, shape, 1) < LANES // 2


def swap(x):
    return pltpu.roll(x, LANES // 2, 1)


def stack_rotated(g):
    other = swap(g)
    return jnp.concatenate([g, jnp.where(first_half(g.shape), -other, other)], axis=0)


def site_kernel(strength_ref, weight_ref, fh_ref, fl_ref, bh_ref, bl_ref, x_ref, *refs):
    y_ref = refs[-1]
    momenta, _, rows, _ = x_ref.shape
    x, y = x_ref.reshape(-1, LANES), y_ref.reshape(-1, LANES)
    left = first_half((K, LANES))
    weight = weight_ref[...]
    scale = -strength_ref[0]

    def place(spin, row):
        return pl.ds(spin * rows + row, momenta, stride=2 * rows), slice(None)

    @pl.loop(0, rows // 2)
    def _(pair):
        site = []
        for spin in range(2):
            a, b = x[place(spin, 2 * pair)], x[place(spin, 2 * pair + 1)]
            re = jnp.where(left, a, swap(b))
            im = jnp.where(left, swap(a), b)
            joined = split(jnp.concatenate([re, im], axis=1))
            out = dot3((fh_ref[...], fl_ref[...]), joined)
            c_re, c_im = out[:K, :LANES], out[:K, LANES:]
            s_re, s_im = out[K:, :LANES], out[K:, LANES:]
            site.append((c_re - s_im, c_im + s_re, c_re + s_im, c_im - s_re))
        (r0, i0, *_), (r1, i1, *_) = site
        pair_re = scale * (r0 * r1 - i0 * i1)
        pair_im = scale * (r0 * i1 + i0 * r1)
        for spin in range(2):
            _, _, m_re, m_im = site[1 - spin]
            sig_re = pair_re * m_re + pair_im * m_im
            sig_im = pair_im * m_re - pair_re * m_im
            joined = split(jnp.concatenate([sig_re, sig_im], axis=1))
            out = dot3((bh_ref[...], bl_ref[...]), joined)
            re = (out[:K, :LANES] + out[K:, LANES:]) * weight
            im = (out[:K, LANES:] - out[K:, :LANES]) * weight
            y[place(spin, 2 * pair)] = jnp.where(left, re, swap(im))
            y[place(spin, 2 * pair + 1)] = jnp.where(left, swap(re), im)


def site_sigma(strength, weights, tables, x, after=()):
    vmem = pl.BlockSpec(memory_space=pltpu.VMEM)
    return pl.pallas_call(
        site_kernel,
        out_shape=jax.ShapeDtypeStruct(x.shape, f32),
        in_specs=[pl.BlockSpec(memory_space=pltpu.SMEM)] + [vmem] * 6 + unread(after),
        out_specs=vmem,
        compiler_params=pltpu.CompilerParams(vmem_limit_bytes=VMEM_LIMIT),
        cost_estimate=SMALL,
        name="site_sigma",
    )(strength, weights, *tables, x, *after)


def unread(after):
    return [pl.BlockSpec(memory_space=pl.ANY)] * len(after)


def conv_kernel(parts, info_ref, s_ref, *refs):
    g_refs, c_ref = refs[:parts], refs[-1]
    for k in range(c_ref.shape[0]):
        for spin in range(2):
            s = split(jnp.concatenate([s_ref[z, k, spin] for z in range(s_ref.shape[0])], axis=0))
            g = jnp.concatenate([x[k, spin] for x in g_refs], axis=0)
            c_ref[k, spin] = -dot3(s, split(stack_rotated(g)), transposed=True)


def moved_by(info_ref_at=0):
    return lambda i, info: (info[info_ref_at] + i, 0, 0, 0)


def still(i, info):
    return (i, 0, 0, 0)


def cut_block(shape):
    return pl.BlockSpec((shape[0], KBLOCK, *shape[2:]), lambda i, info: (0, info[0] + i, 0, 0, 0))


def conv_rows(info, sigma, g_parts, kcount, after=()):
    total = sigma.shape[0] * sigma.shape[3]
    return pl.pallas_call(
        functools.partial(conv_kernel, len(g_parts)),
        out_shape=jax.ShapeDtypeStruct((kcount, 2, total, LANES), f32),
        grid_spec=pltpu.PrefetchScalarGridSpec(
            num_scalar_prefetch=1,
            grid=(kcount // KBLOCK,),
            in_specs=[cut_block(sigma.shape)]
            + [pl.BlockSpec((KBLOCK, *x.shape[1:]), moved_by()) for x in g_parts]
            + unread(after),
            out_specs=pl.BlockSpec((KBLOCK, 2, total, LANES), still),
        ),
        compiler_params=pltpu.CompilerParams(vmem_limit_bytes=VMEM_LIMIT),
        cost_estimate=SMALL,
        name="conv_rows",
    )(info, sigma, *g_parts, *after)


def update_kernel(outs, parts, step_scale, info_ref, c_ref, start_ref, *refs):
    g_refs, out_refs = refs[:parts], refs[len(refs) - outs :]
    now_ref, cut_refs = out_refs[0], out_refs[1:]
    for k in range(now_ref.shape[0]):
        for spin in range(2):
            c = split(c_ref[k, spin])
            g = jnp.concatenate([x[k, spin] for x in g_refs], axis=0)
            new = start_ref[k, spin] + step_scale * dot3(c, split(stack_rotated(g)))
            now_ref[k, spin] = new
            for cut in cut_refs:
                count, rows = cut.shape[0], cut.shape[3]
                for z in range(count):
                    cut[z, k, spin] = new[z * rows : (z + 1) * rows]


def update_rows(info, conv, panel_start, g_parts, chunk, count, step_scale, cuts, previous=(), after=()):
    momenta, spins, panel, _ = panel_start.shape
    total = conv.shape[2]
    shapes = [jax.ShapeDtypeStruct((momenta, spins, total, LANES), f32)]
    specs = [pl.BlockSpec((KBLOCK, spins, total, LANES), moved_by())]
    if cuts:
        shape = (count, momenta, spins, total // count, LANES)
        shapes.append(jax.ShapeDtypeStruct(shape, f32))
        specs.append(cut_block(shape))
    first = 1 + 2 + len(g_parts)
    return pl.pallas_call(
        functools.partial(update_kernel, len(shapes), len(g_parts), step_scale),
        out_shape=shapes,
        grid_spec=pltpu.PrefetchScalarGridSpec(
            num_scalar_prefetch=1,
            grid=(conv.shape[0] // KBLOCK,),
            in_specs=[
                pl.BlockSpec((KBLOCK, spins, total, LANES), still),
                pl.BlockSpec((KBLOCK, spins, total, LANES), lambda i, info: (info[0] + i, 0, chunk, 0)),
            ]
            + [pl.BlockSpec((KBLOCK, *g.shape[1:]), moved_by()) for g in g_parts]
            + unread(previous)
            + unread(after),
            out_specs=specs,
        ),
        input_output_aliases={first + i: i for i in range(len(previous))},
        compiler_params=pltpu.CompilerParams(vmem_limit_bytes=VMEM_LIMIT),
        cost_estimate=SMALL,
        name="update_rows",
    )(info, conv, panel_start, *g_parts, *previous, *after)


def final_kernel(chunks, shares, step_scale, info_ref, *refs):
    c_refs, start_ref = refs[:chunks], refs[chunks]
    now_refs = refs[chunks + 1 : 2 * chunks]
    g_refs = refs[2 * chunks : 3 * chunks]
    d_refs, out_ref = refs[3 * chunks : 3 * chunks + shares], refs[-1]
    total = start_ref.shape[2]

    @pl.when(info_ref[3] == 0)
    def _():
        for k in range(out_ref.shape[0]):
            for spin in range(2):
                g = jnp.concatenate([x[k, spin] for x in g_refs], axis=0)
                moved = dot3(split(c_refs[-1][k, spin]), split(stack_rotated(g)))
                for chunk, now in enumerate(now_refs):
                    out_ref[k, spin, pl.ds(chunk * total, total), :] = now[k, spin]
                out_ref[k, spin, pl.ds((chunks - 1) * total, total), :] = start_ref[k, spin] + step_scale * moved

    @pl.when(info_ref[3] == 1)
    def _():
        rows = d_refs[0].shape[2]
        for k in range(out_ref.shape[0]):
            for spin in range(2):
                d = jnp.concatenate([x[k, spin] for x in d_refs], axis=0)
                c = jnp.concatenate([x[k, spin] for x in c_refs], axis=0)
                block = d + step_scale * dot3(split(d), split(stack_rotated(c)))
                for e in range(shares):
                    at = pl.ds(pl.multiple_of((info_ref[1] ^ e) * rows, rows), rows)
                    out_ref[k, spin, at, :] = block[e * rows : (e + 1) * rows]


def final_rows(info, convs, panel_start, nows, g_parts, guess, step_scale, previous=()):
    momenta, spins, panel, _ = panel_start.shape
    chunks, total = len(convs), convs[0].shape[2]
    picked = lambda i, info: (info[3] * i, 0, 0, 0)
    picked_moved = lambda i, info: (info[3] * (info[0] + i), 0, 0, 0)
    c_block = (KBLOCK, spins, total, LANES)
    first = 1 + 3 * chunks + len(guess)
    return pl.pallas_call(
        functools.partial(final_kernel, chunks, len(guess), step_scale),
        out_shape=jax.ShapeDtypeStruct(panel_start.shape, f32),
        grid_spec=pltpu.PrefetchScalarGridSpec(
            num_scalar_prefetch=1,
            grid=(convs[0].shape[0] // KBLOCK,),
            in_specs=[pl.BlockSpec(c_block, picked)] * (chunks - 1)
            + [pl.BlockSpec(c_block, still)]
            + [pl.BlockSpec(c_block, lambda i, info: (info[0] + i, 0, chunks - 1, 0))]
            + [pl.BlockSpec(c_block, moved_by())] * (chunks - 1)
            + [pl.BlockSpec((KBLOCK, *g.shape[1:]), moved_by()) for g in g_parts]
            + [pl.BlockSpec((KBLOCK, *x.shape[1:]), picked_moved) for x in guess]
            + unread(previous),
            out_specs=pl.BlockSpec((KBLOCK, spins, panel, LANES), moved_by()),
        ),
        input_output_aliases={first + i: i for i in range(len(previous))},
        compiler_params=pltpu.CompilerParams(vmem_limit_bytes=VMEM_LIMIT),
        cost_estimate=SMALL,
        name="final_rows",
    )(info, *convs, panel_start, *nows, *g_parts, *guess, *previous)


def add_kernel(a_ref, b_ref, *refs):
    refs[-1][...] = a_ref[...] + b_ref[...]


def added(a, b, after=()):
    block = pl.BlockSpec((KBLOCK, *a.shape[1:]), lambda i: (i, 0, 0, 0))
    return pl.pallas_call(
        add_kernel,
        out_shape=jax.ShapeDtypeStruct(a.shape, f32),
        grid=(a.shape[0] // KBLOCK,),
        in_specs=[block, block] + unread(after),
        out_specs=block,
        cost_estimate=SMALL,
        name="added",
    )(a, b, *after)


def pairs(size, d):
    return [(i, i ^ d) for i in range(size)]


def exchange(cut):
    return lax.all_to_all(cut, "mom", split_axis=0, concat_axis=0, tiled=True)


def table_parts(ordering):
    cos_table, sin_table = phases(ordering)
    out = []
    for table in (
        jnp.concatenate([cos_table, sin_table], axis=0),
        jnp.concatenate([cos_table.T, sin_table.T], axis=0),
    ):
        high = lax.reduce_precision(table, exponent_bits=8, mantissa_bits=7)
        out += [high.astype(bf16), (table - high).astype(bf16)]
    return out


def body(panel_start, block_guess, coupling, slab_owner, expiring, ordering):
    momenta, spins, panel, _ = panel_start.shape
    count, slabs = lax.axis_size("mom"), lax.axis_size("tm")
    my_tm = lax.axis_index("tm")
    weights, chosen = window_weights(slab_owner, expiring, my_tm, slabs, panel)
    weights = weights.reshape(1, LANES)
    strength = coupling * coupling
    step_scale = 1.0 / math.sqrt(panel)
    total = panel // CHUNKS
    rows = total // count
    half = momenta // 2
    core = my_tm % 2
    flag = chosen.astype(jnp.int32)

    def info(k_half):
        return jnp.stack([k_half * (half // KBLOCK), my_tm, core, flag]).astype(jnp.int32)

    infos = (info(core), info(1 - core))

    def cut(chunk):
        part = panel_start[:, :, chunk * total : (chunk + 1) * total]
        return part.reshape(momenta, spins, count, rows, LANES).transpose(2, 0, 1, 3, 4)

    def gathered(x):
        out, bit = [x], slabs // 2
        gaps = [0]
        while bit:
            out += [lax.ppermute(y, "tm", pairs(slabs, bit)) for y in out]
            gaps += [g ^ bit for g in gaps]
            bit //= 2
        return [y for _, y in sorted(zip(gaps, out), key=lambda both: both[0])]

    def convolved(blocks, g_parts, after, between=lambda keep: ()):
        give = conv_rows(infos[1], blocks, g_parts, half, after)
        keep = conv_rows(infos[0], blocks, g_parts, half, (give,))
        beside = between(keep)
        mine = keep + lax.ppermute(give, "tm", pairs(slabs, 1))
        bit = 2
        while bit < slabs:
            mine = added(mine, lax.ppermute(mine, "tm", pairs(slabs, bit)), beside)
            bit *= 2
        return mine, lax.ppermute(mine, "tm", pairs(slabs, 1)), beside

    def updated(conv, g_parts, chunk, blocks, after=()):
        out = ()
        for which in range(2):
            out = update_rows(
                infos[which], conv[which], panel_start, g_parts, chunk, count, step_scale, blocks, out, after
            )
            after = ()
        return out

    sent = [cut(c) for c in range(CHUNKS)]
    tables = table_parts(ordering)
    guess = gathered(block_guess)
    g_parts = [panel_start]
    before = tuple(guess)
    for sweep in range(PASSES):
        last = sweep == PASSES - 1
        arrived = [exchange(x) for x in sent]
        sigma = []
        for chunk in range(CHUNKS):
            site = arrived[chunk].reshape(K, spins, rows, LANES)
            out = site_sigma(strength, weights, tables, site, before)
            before = (out,)
            sigma.append(exchange(out.reshape(count, momenta, spins, rows, LANES)))
        convs, news = [], []
        for chunk in range(CHUNKS):
            beside = lambda keep: ()
            if last and chunk == CHUNKS - 1:
                beside = lambda keep: [
                    updated(convs[c], g_parts, c, False, (keep,))[0] for c in range(CHUNKS - 1)
                ]
            mine, other, nows = convolved(sigma[chunk], g_parts, before, beside)
            convs.append((mine, other))
            before = (mine,)
            if not last:
                news.append(updated((mine, other), g_parts, chunk, True))
                before = (news[-1][0],)
        if not last:
            g_parts = [n[0] for n in news]
            sent = [n[1] for n in news]
    out = ()
    for which in range(2):
        halves = [c[which] for c in convs]
        out = (final_rows(infos[which], halves, panel_start, nows, g_parts, guess, step_scale, out),)
    return out[0]


def fits(mesh):
    def tiled(panel_start, *_):
        momenta, spins, panel, width = panel_start.shape
        count, slabs = mesh.shape["mom"], mesh.shape["tm"]
        powers = all(n & (n - 1) == 0 for n in (count, slabs))
        local = momenta // count
        return (
            powers
            and slabs > 1
            and spins == 2 * mesh.shape["groups"]
            and width == LANES * slabs
            and 2 * panel == LANES
            and panel == CHUNKS * count * ROWS
            and local % (2 * KBLOCK) == 0
            and PASSES == 2
        )

    return tiled


def solution(mesh):
    def mapped(inner):
        return jax.shard_map(
            inner,
            mesh=mesh,
            in_specs=(
                P("mom", "groups", None, "tm"),
                P("mom", "groups", "tm", None),
                P("groups"),
                P("groups"),
                P("groups"),
                P(),
            ),
            out_specs=P("mom", "groups", None, "tm"),
            check_vma=False,
        )

    def chosen(*args):
        return mapped(body if fits(mesh)(*args) else plain_body)(*args)

    return chosen
```

```python
import functools
import math

import jax
import jax.numpy as jnp
from jax import lax
from jax.experimental import pallas as pl
from jax.experimental.pallas import tpu as pltpu
from jax.sharding import PartitionSpec as P

LSIDE = 16
K = 256
PASSES = 2
CHUNKS = 2
PIECES = 2
ROWS = 8
LANES = 128
KBLOCK = 8
VMEM_LIMIT = 48 * 2**20
f32, bf16 = jnp.float32, jnp.bfloat16
SMALL = pl.CostEstimate(flops=1, bytes_accessed=1, transcendentals=0)


def window_weights(slab_owner, expiring, own_index, slab_count, panel):
    blocks = jnp.arange(slab_count, dtype=jnp.int32)
    slab_mine = jnp.sum(blocks * (slab_owner == own_index).astype(jnp.int32))
    position = (slab_mine - expiring[0]) % slab_count
    window = slab_count * panel
    times = position * panel + jnp.arange(panel, dtype=jnp.int32)
    weights = jnp.exp(-1.5 * (window - 1 - times).astype(f32) / window) / math.sqrt(window)
    owner_expiring = jnp.sum(slab_owner * (blocks == expiring[0]).astype(jnp.int32))
    return jnp.concatenate([weights, weights]), own_index == owner_expiring


def phases(ordering):
    site = jnp.arange(K, dtype=jnp.int32)
    turn = (
        (site // LSIDE)[:, None] * (ordering // LSIDE)[None, :]
        + (site % LSIDE)[:, None] * (ordering % LSIDE)[None, :]
    ) % LSIDE
    angles = turn.astype(f32) * (2.0 * math.pi / LSIDE)
    return jnp.cos(angles) / LSIDE, jnp.sin(angles) / LSIDE


def product(left, right):
    return jnp.dot(left, right, precision=lax.Precision.HIGHEST, preferred_element_type=f32)


def contract(pattern, left, right):
    return jnp.einsum(
        pattern, left, right, precision=lax.Precision.HIGHEST, preferred_element_type=f32
    )


def rotated(joined):
    half = joined.shape[-1] // 2
    return jnp.concatenate([-joined[..., half:], joined[..., :half]], axis=-1)


def plain_sigma(joined, cos_table, sin_table, strength):
    layout, half = joined.shape, joined.shape[-1] // 2
    flat = joined.reshape(K, -1)
    with_cos = product(cos_table, flat).reshape(layout)
    with_sin = product(sin_table, flat).reshape(layout)
    c_re, c_im = with_cos[..., :half], with_cos[..., half:]
    s_re, s_im = with_sin[..., :half], with_sin[..., half:]
    site_re, site_im = c_re - s_im, c_im + s_re
    back_re, back_im = (c_re + s_im)[:, ::-1], (c_im - s_re)[:, ::-1]
    other_re, other_im = site_re[:, ::-1], site_im[:, ::-1]
    pair_re = site_re * other_re - site_im * other_im
    pair_im = site_re * other_im + site_im * other_re
    sig_re = -strength * (pair_re * back_re + pair_im * back_im)
    sig_im = -strength * (pair_im * back_re - pair_re * back_im)
    sig = jnp.concatenate([sig_re, sig_im], axis=-1).reshape(K, -1)
    back_cos = product(cos_table.T, sig).reshape(layout)
    back_sin = product(sin_table.T, sig).reshape(layout)
    out_re = back_cos[..., :half] + back_sin[..., half:]
    out_im = back_cos[..., half:] - back_sin[..., :half]
    return jnp.concatenate([out_re, out_im], axis=-1)


def plain_body(panel_start, block_guess, coupling, slab_owner, expiring, ordering):
    panel = panel_start.shape[2]
    weights, chosen = window_weights(
        slab_owner, expiring, lax.axis_index("tm"), lax.axis_size("tm"), panel
    )
    cos_table, sin_table = phases(ordering)
    strength = coupling[0] * coupling[0]
    step_scale = 1.0 / math.sqrt(panel)
    guess = lax.all_gather(block_guess, "tm", axis=2, tiled=True)
    current = panel_start
    for _ in range(PASSES):
        exchanged = lax.all_to_all(current, "mom", split_axis=2, concat_axis=0, tiled=True)
        sigma = plain_sigma(exchanged, cos_table, sin_table, strength)
        returned = lax.all_to_all(sigma, "mom", split_axis=0, concat_axis=2, tiled=True)
        stacked = jnp.concatenate([current, rotated(current)], axis=2)
        conv = lax.psum(-contract("ksau,ksbu->ksab", returned * weights, stacked), "tm")
        current = panel_start + step_scale * contract("ksab,ksbu->ksau", conv, stacked)
    stacked = jnp.concatenate([conv, rotated(conv)], axis=2)
    block = guess + step_scale * contract("ksab,ksbc->ksac", guess, stacked)
    return jnp.where(chosen, block, current)


def split(x):
    high = x.astype(bf16)
    return high, (x - high.astype(f32)).astype(bf16)


def dot(left, right, transposed=False):
    dims = (((1,), (1 if transposed else 0,)), ((), ()))
    return lax.dot_general(left, right, dims, preferred_element_type=f32)


def dot3(left, right, transposed=False):
    (lh, ll), (rh, rl) = left, right
    rows = lh.shape[0]
    both = dot(jnp.concatenate([lh, ll], axis=0), rh, transposed)
    return both[:rows] + (both[rows:] + dot(lh, rl, transposed))


def dot_spins(lefts, rights, transposed=False):
    rows = lefts[0].shape[0]
    left = []
    for x in lefts:
        high, low = split(x)
        left += [jnp.concatenate([high, high], axis=1), jnp.concatenate([low, jnp.zeros_like(low)], axis=1)]
    parts = [split(x) for x in rights]
    along, across = (1, 0) if transposed else (0, 1)
    right = jnp.concatenate([jnp.concatenate(p, axis=along) for p in parts], axis=across)
    out = dot(jnp.concatenate(left, axis=0), right, transposed)
    return [
        out[2 * i * rows : (2 * i + 1) * rows, i * LANES : (i + 1) * LANES]
        + out[(2 * i + 1) * rows : (2 * i + 2) * rows, i * LANES : (i + 1) * LANES]
        for i in range(2)
    ]


def first_half(shape):
    return lax.broadcasted_iota(jnp.int32, shape, 1) < LANES // 2


def swap(x):
    return pltpu.roll(x, LANES // 2, 1)


def stack_rotated(g):
    other = swap(g)
    return jnp.concatenate([g, jnp.where(first_half(g.shape), -other, other)], axis=0)


def site_kernel(pieces, count, strength_ref, weight_ref, fh_ref, fl_ref, bh_ref, bl_ref, x_ref, *refs):
    momenta, _, rows, _ = x_ref.shape
    x = x_ref.reshape(-1, LANES)
    outs = [y.reshape(-1, LANES) for y in refs[len(refs) - 1 - pieces : -1]]
    left = first_half((K, LANES))
    weight = weight_ref[...]
    scale = -strength_ref[0]

    def place(spin, row, momenta=momenta):
        return pl.ds(spin * rows + row, momenta, stride=2 * rows), slice(None)

    def put(spin, row, value):
        step = momenta // (pieces * count)
        for j, y in enumerate(outs):
            at = [(z * pieces + j) * step for z in range(count)]
            part = jnp.concatenate([value[i : i + step] for i in at], axis=0) if pieces > 1 else value
            y[place(spin, row, momenta // pieces)] = part

    @pl.loop(0, rows // 2)
    def _(pair):
        site = []
        for spin in range(2):
            a, b = x[place(spin, 2 * pair)], x[place(spin, 2 * pair + 1)]
            re = jnp.where(left, a, swap(b))
            im = jnp.where(left, swap(a), b)
            joined = split(jnp.concatenate([re, im], axis=1))
            out = dot3((fh_ref[...], fl_ref[...]), joined)
            c_re, c_im = out[:K, :LANES], out[:K, LANES:]
            s_re, s_im = out[K:, :LANES], out[K:, LANES:]
            site.append((c_re - s_im, c_im + s_re, c_re + s_im, c_im - s_re))
        (r0, i0, *_), (r1, i1, *_) = site
        pair_re = scale * (r0 * r1 - i0 * i1)
        pair_im = scale * (r0 * i1 + i0 * r1)
        for spin in range(2):
            _, _, m_re, m_im = site[1 - spin]
            sig_re = pair_re * m_re + pair_im * m_im
            sig_im = pair_im * m_re - pair_re * m_im
            joined = split(jnp.concatenate([sig_re, sig_im], axis=1))
            out = dot3((bh_ref[...], bl_ref[...]), joined)
            re = (out[:K, :LANES] + out[K:, LANES:]) * weight
            im = (out[:K, LANES:] - out[K:, :LANES]) * weight
            put(spin, 2 * pair, jnp.where(left, re, swap(im)))
            put(spin, 2 * pair + 1, jnp.where(left, swap(re), im))


def site_sigma(strength, weights, tables, x, count, pieces, after=()):
    vmem = pl.BlockSpec(memory_space=pltpu.VMEM)
    shape = (x.shape[0] // pieces, *x.shape[1:])
    return pl.pallas_call(
        functools.partial(site_kernel, pieces, count),
        out_shape=[pltpu.HBM(shape, f32)] * pieces + [MARK],
        in_specs=[pl.BlockSpec(memory_space=pltpu.SMEM)] + [vmem] * 6 + unread(after),
        out_specs=[vmem] * pieces + [MARK_SPEC],
        compiler_params=pltpu.CompilerParams(vmem_limit_bytes=VMEM_LIMIT),
        cost_estimate=SMALL,
        name="site_sigma",
    )(strength, weights, *tables, x, *after)


def cut_kernel(x_ref, y_ref):
    count, _, _, rows, _ = y_ref.shape
    for z in range(count):
        y_ref[z] = x_ref[:, :, z * rows : (z + 1) * rows, :]


def cut_rows(panel_start, chunk, total, count):
    momenta, spins = panel_start.shape[:2]
    step = momenta // 4
    return pl.pallas_call(
        cut_kernel,
        out_shape=pltpu.HBM((count, momenta, spins, total // count, LANES), f32),
        grid=(4,),
        in_specs=[pl.BlockSpec((step, spins, total, LANES), lambda i: (i, 0, chunk, 0))],
        out_specs=pl.BlockSpec((count, step, spins, total // count, LANES), lambda i: (0, i, 0, 0, 0)),
        compiler_params=pltpu.CompilerParams(vmem_limit_bytes=VMEM_LIMIT),
        cost_estimate=SMALL,
        name="cut_rows",
    )(panel_start)


def unread(after):
    return [pl.BlockSpec(memory_space=pl.ANY)] * len(after)


MARK = jax.ShapeDtypeStruct((8, LANES), f32)
MARK_SPEC = pl.BlockSpec(memory_space=pl.ANY)


def mark_of(x):
    return x[0, 0, :8]


def stacks(refs, k):
    return [stack_rotated(jnp.concatenate([x[k, spin] for x in refs], axis=0)) for spin in range(2)]


def conv_kernel(parts, info_ref, s_ref, *refs):
    g_refs, c_ref = refs[:parts], refs[-2]
    for k in range(c_ref.shape[0]):
        sigma = [jnp.concatenate([s_ref[z, k, spin] for z in range(s_ref.shape[0])], axis=0) for spin in range(2)]
        out = dot_spins(sigma, stacks(g_refs, k), transposed=True)
        for spin in range(2):
            c_ref[k, spin] = -out[spin]


def moved_by(info_ref_at=0):
    return lambda i, info: (info[info_ref_at] + i, 0, 0, 0)


def still(i, info):
    return (i, 0, 0, 0)


def cut_block(shape, at=0):
    return pl.BlockSpec((shape[0], KBLOCK, *shape[2:]), lambda i, info: (0, info[at] + i, 0, 0, 0))


def conv_rows(info, sigma, g_parts, kcount, whole, after=()):
    total = sigma.shape[0] * sigma.shape[3]
    return pl.pallas_call(
        functools.partial(conv_kernel, len(g_parts)),
        out_shape=[jax.ShapeDtypeStruct((kcount, 2, total, LANES), f32), MARK],
        grid_spec=pltpu.PrefetchScalarGridSpec(
            num_scalar_prefetch=1,
            grid=(kcount // KBLOCK,),
            in_specs=[cut_block(sigma.shape, 0 if whole else 4)]
            + [pl.BlockSpec((KBLOCK, *x.shape[1:]), moved_by()) for x in g_parts]
            + unread(after),
            out_specs=[pl.BlockSpec((KBLOCK, 2, total, LANES), still), MARK_SPEC],
        ),
        compiler_params=pltpu.CompilerParams(vmem_limit_bytes=VMEM_LIMIT),
        cost_estimate=SMALL,
        name="conv_rows",
    )(info, sigma, *g_parts, *after)


def update_kernel(outs, parts, step_scale, info_ref, mine_ref, other_ref, start_ref, *refs):
    g_refs, out_refs = refs[:parts], refs[len(refs) - 1 - outs : -1]
    now_ref, cut_refs = out_refs[0], out_refs[1:]
    own = pl.program_id(0) // (pl.num_programs(0) // 2) == info_ref[2]
    for k in range(now_ref.shape[0]):
        conv = [jnp.where(own, mine_ref[k, spin], other_ref[k, spin]) for spin in range(2)]
        moved = dot_spins(conv, stacks(g_refs, k))
        for spin in range(2):
            new = start_ref[k, spin] + step_scale * moved[spin]
            now_ref[k, spin] = new
            for cut in cut_refs:
                count, rows = cut.shape[0], cut.shape[3]
                for z in range(count):
                    cut[z, k, spin] = new[z * rows : (z + 1) * rows]


def update_rows(info, conv, panel_start, g_parts, chunk, count, step_scale, cuts, previous=(), after=()):
    momenta, spins, panel, _ = panel_start.shape
    part, _, total, _ = conv[0].shape
    steps = part // KBLOCK
    of_piece = moved_by(5)
    shapes = [jax.ShapeDtypeStruct((momenta, spins, total, LANES), f32)]
    specs = [pl.BlockSpec((KBLOCK, spins, total, LANES), of_piece)]
    if cuts:
        shape = (count, momenta, spins, total // count, LANES)
        shapes.append(pltpu.HBM(shape, f32))
        specs.append(cut_block(shape, 5))
    first = 1 + 3 + len(g_parts)

    def half(side):
        return lambda i, info: (jnp.clip(i - steps * abs(side - info[2]), 0, steps - 1), 0, 0, 0)

    return pl.pallas_call(
        functools.partial(update_kernel, len(shapes), len(g_parts), step_scale),
        out_shape=shapes + [MARK],
        grid_spec=pltpu.PrefetchScalarGridSpec(
            num_scalar_prefetch=1,
            grid=(2 * steps,),
            in_specs=[
                pl.BlockSpec((KBLOCK, spins, total, LANES), half(0)),
                pl.BlockSpec((KBLOCK, spins, total, LANES), half(1)),
                pl.BlockSpec((KBLOCK, spins, total, LANES), lambda i, info: (info[5] + i, 0, chunk, 0)),
            ]
            + [pl.BlockSpec((KBLOCK, *g.shape[1:]), of_piece) for g in g_parts]
            + unread(previous)
            + unread(after),
            out_specs=specs + [MARK_SPEC],
        ),
        input_output_aliases={first + i: i for i in range(len(previous))},
        compiler_params=pltpu.CompilerParams(vmem_limit_bytes=VMEM_LIMIT),
        cost_estimate=SMALL,
        name="update_rows",
    )(info, *conv, panel_start, *g_parts, *previous, *after)


def final_kernel(chunks, shares, step_scale, info_ref, *refs):
    c_refs, start_ref = refs[:chunks], refs[chunks]
    now_refs = refs[chunks + 1 : 2 * chunks]
    g_refs = refs[2 * chunks : 3 * chunks]
    d_refs, out_ref = refs[3 * chunks : 3 * chunks + shares], refs[-2]
    total = start_ref.shape[2]

    @pl.when(info_ref[3] == 0)
    def _():
        for k in range(out_ref.shape[0]):
            moved = dot_spins([c_refs[-1][k, spin] for spin in range(2)], stacks(g_refs, k))
            for spin in range(2):
                for chunk, now in enumerate(now_refs):
                    out_ref[k, spin, pl.ds(chunk * total, total), :] = now[k, spin]
                out_ref[k, spin, pl.ds((chunks - 1) * total, total), :] = start_ref[k, spin] + step_scale * moved[spin]

    @pl.when(info_ref[3] == 1)
    def _():
        rows = d_refs[0].shape[2]
        for k in range(out_ref.shape[0]):
            guess = [jnp.concatenate([x[k, spin] for x in d_refs], axis=0) for spin in range(2)]
            moved = dot_spins(guess, stacks(c_refs, k))
            for spin in range(2):
                block = guess[spin] + step_scale * moved[spin]
                for e in range(shares):
                    at = pl.ds(pl.multiple_of((info_ref[1] ^ e) * rows, rows), rows)
                    out_ref[k, spin, at, :] = block[e * rows : (e + 1) * rows]


def final_rows(info, convs, panel_start, nows, g_parts, guess, step_scale, previous=(), after=()):
    momenta, spins, panel, _ = panel_start.shape
    chunks, total = len(convs), convs[0].shape[2]
    picked = lambda i, info: (info[3] * i, 0, 0, 0)
    picked_moved = lambda i, info: (info[3] * (info[0] + i), 0, 0, 0)
    c_block = (KBLOCK, spins, total, LANES)
    first = 1 + 3 * chunks + len(guess)
    return pl.pallas_call(
        functools.partial(final_kernel, chunks, len(guess), step_scale),
        out_shape=[jax.ShapeDtypeStruct(panel_start.shape, f32), MARK],
        grid_spec=pltpu.PrefetchScalarGridSpec(
            num_scalar_prefetch=1,
            grid=(convs[0].shape[0] // KBLOCK,),
            in_specs=[pl.BlockSpec(c_block, picked)] * (chunks - 1)
            + [pl.BlockSpec(c_block, still)]
            + [pl.BlockSpec(c_block, lambda i, info: (info[0] + i, 0, chunks - 1, 0))]
            + [pl.BlockSpec(c_block, moved_by())] * (chunks - 1)
            + [pl.BlockSpec((KBLOCK, *g.shape[1:]), moved_by()) for g in g_parts]
            + [pl.BlockSpec((KBLOCK, *x.shape[1:]), picked_moved) for x in guess]
            + unread(previous)
            + unread(after),
            out_specs=[pl.BlockSpec((KBLOCK, spins, panel, LANES), moved_by()), MARK_SPEC],
        ),
        input_output_aliases={first + i: i for i in range(len(previous))},
        compiler_params=pltpu.CompilerParams(vmem_limit_bytes=VMEM_LIMIT),
        cost_estimate=SMALL,
        name="final_rows",
    )(info, *convs, panel_start, *nows, *g_parts, *guess, *previous, *after)


def add_kernel(a_ref, b_ref, *refs):
    refs[-2][...] = a_ref[...] + b_ref[...]


def added(a, b, after=()):
    vmem = pl.BlockSpec(memory_space=pltpu.VMEM)
    return pl.pallas_call(
        add_kernel,
        out_shape=[jax.ShapeDtypeStruct(a.shape, f32), MARK],
        in_specs=[vmem, vmem] + unread(after),
        out_specs=[vmem, MARK_SPEC],
        cost_estimate=SMALL,
        name="added",
    )(a, b, *after)


def pairs(size, d):
    return [(i, i ^ d) for i in range(size)]


def exchange(cut):
    return lax.all_to_all(cut, "mom", split_axis=0, concat_axis=0, tiled=True)


def table_parts(ordering):
    cos_table, sin_table = phases(ordering)
    out = []
    for table in (
        jnp.concatenate([cos_table, sin_table], axis=0),
        jnp.concatenate([cos_table.T, sin_table.T], axis=0),
    ):
        high = lax.reduce_precision(table, exponent_bits=8, mantissa_bits=7)
        out += [high.astype(bf16), (table - high).astype(bf16)]
    return out


def body(panel_start, block_guess, coupling, slab_owner, expiring, ordering):
    momenta, spins, panel, _ = panel_start.shape
    count, slabs = lax.axis_size("mom"), lax.axis_size("tm")
    my_tm = lax.axis_index("tm")
    weights, chosen = window_weights(slab_owner, expiring, my_tm, slabs, panel)
    weights = weights.reshape(1, LANES)
    strength = coupling * coupling
    step_scale = 1.0 / math.sqrt(panel)
    total = panel // CHUNKS
    rows = total // count
    piece = momenta // PIECES
    part = piece // 2
    core = my_tm % 2
    flag = chosen.astype(jnp.int32)

    def info(j, side):
        own, at = side * (part // KBLOCK), j * (piece // KBLOCK)
        return jnp.stack([at + own, my_tm, core, flag, own, at]).astype(jnp.int32)

    infos = [(info(j, core), info(j, 1 - core)) for j in range(PIECES)]

    def gathered(x):
        out, gaps, bit = [x], [0], slabs // 2
        while bit:
            out += [lax.ppermute(y, "tm", pairs(slabs, bit)) for y in out]
            gaps += [g ^ bit for g in gaps]
            bit //= 2
        return [y for _, y in sorted(zip(gaps, out), key=lambda both: both[0])]

    def convolved(sigma, g_parts, j, after):
        whole = len(sigma) == 1
        source = sigma[0 if whole else j]
        give, given = conv_rows(infos[j][1], source, g_parts, part, whole, after)
        keep, kept = conv_rows(infos[j][0], source, g_parts, part, whole, (given,))
        mine = keep + lax.ppermute(give, "tm", pairs(slabs, 1))
        before = (kept, mark_of(mine))
        bit = 2
        while 2 * bit < slabs:
            mine = mine + lax.ppermute(mine, "tm", pairs(slabs, bit))
            bit *= 2
        return (mine, lax.ppermute(mine, "tm", pairs(slabs, bit))), before

    def summed(two, after=()):
        mine, mark = added(*two, after) if after else (two[0] + two[1], None)
        return (mine, lax.ppermute(mine, "tm", pairs(slabs, 1))), (mark_of(mine) if mark is None else mark,)

    def updated(conv, g_parts, chunk, cuts, after=()):
        out = ()
        for j in range(PIECES):
            *out, mark = update_rows(
                infos[j][0], conv[j], panel_start, g_parts, chunk, count, step_scale, cuts, out, after
            )
            after = ()
        return out, (mark,)

    sent = [cut_rows(panel_start, c, total, count) for c in range(CHUNKS)]
    tables = table_parts(ordering)
    guess = gathered(block_guess)
    g_parts = [panel_start]
    before = tuple(mark_of(x) for x in guess)
    for sweep in range(PASSES):
        last = sweep == PASSES - 1
        arrived = [exchange(x) for x in sent]
        sigma = []
        for chunk in range(CHUNKS):
            site = arrived[chunk].reshape(K, spins, rows, LANES)
            cuts = PIECES if last and chunk == CHUNKS - 1 else 1
            *parts, mark = site_sigma(strength, weights, tables, site, count, cuts, before)
            before = (mark,)
            sigma.append([exchange(x.reshape(count, -1, spins, rows, LANES)) for x in parts])
        convs, news = [], []
        for chunk in range(CHUNKS - 1 if last else CHUNKS):
            twos = []
            for j in range(PIECES):
                two, before = convolved(sigma[chunk], g_parts, j, before)
                twos.append(two)
            sums = [summed(two) for two in twos]
            convs.append([conv for conv, _ in sums])
            before = tuple(mark for _, marks in sums for mark in marks)
            if not last:
                new, before = updated(convs[-1], g_parts, chunk, True)
                news.append(new)
        if not last:
            g_parts = [n[0] for n in news]
            sent = [n[1] for n in news]

    def final_piece(j, conv, out, after):
        for which in range(2):
            halves = [c[j][which] for c in convs] + [conv[which]]
            *out, mark = final_rows(
                infos[j][which], halves, panel_start, nows, g_parts, guess, step_scale, out, after
            )
            after = ()
        return out, (mark,)

    out, nows = (), []
    for j in range(PIECES):
        two, ready = convolved(sigma[-1], g_parts, j, before)
        if j == 0:
            beside = ready
            for c in range(CHUNKS - 1):
                new, beside = updated(convs[c], g_parts, c, False, beside)
                nows.append(new[0])
        else:
            out, beside = final_piece(j - 1, conv, out, ready)
        conv, before = summed(two, beside)
    return final_piece(PIECES - 1, conv, out, ())[0][0]


def fits(mesh):
    def tiled(panel_start, *_):
        momenta, spins, panel, width = panel_start.shape
        count, slabs = mesh.shape["mom"], mesh.shape["tm"]
        powers = all(n & (n - 1) == 0 for n in (count, slabs))
        local = momenta // count
        return (
            powers
            and slabs > 2
            and spins == 2 * mesh.shape["groups"]
            and width == LANES * slabs
            and 2 * panel == LANES
            and panel == CHUNKS * count * ROWS
            and local % (2 * PIECES * KBLOCK) == 0
            and PASSES == 2
        )

    return tiled


def solution(mesh):
    def mapped(inner):
        return jax.shard_map(
            inner,
            mesh=mesh,
            in_specs=(
                P("mom", "groups", None, "tm"),
                P("mom", "groups", "tm", None),
                P("groups"),
                P("groups"),
                P("groups"),
                P(),
            ),
            out_specs=P("mom", "groups", None, "tm"),
            check_vma=False,
        )

    def chosen(*args):
        return mapped(body if fits(mesh)(*args) else plain_body)(*args)

    return chosen
```

```python
import functools
import math

import jax
import jax.numpy as jnp
from jax import lax
from jax.experimental import pallas as pl
from jax.experimental.pallas import tpu as pltpu
from jax.sharding import PartitionSpec as P

LSIDE = 16
K = 256
PASSES = 2
CHUNKS = 2
PIECES = 2
ROWS = 8
LANES = 128
KBLOCK = 8
WIDE = 2
VMEM_LIMIT = 48 * 2**20
f32, bf16 = jnp.float32, jnp.bfloat16
SMALL = pl.CostEstimate(flops=1, bytes_accessed=1, transcendentals=0)


def window_weights(slab_owner, expiring, own_index, slab_count, panel):
    blocks = jnp.arange(slab_count, dtype=jnp.int32)
    slab_mine = jnp.sum(blocks * (slab_owner == own_index).astype(jnp.int32))
    position = (slab_mine - expiring[0]) % slab_count
    window = slab_count * panel
    times = position * panel + jnp.arange(panel, dtype=jnp.int32)
    weights = jnp.exp(-1.5 * (window - 1 - times).astype(f32) / window) / math.sqrt(window)
    owner_expiring = jnp.sum(slab_owner * (blocks == expiring[0]).astype(jnp.int32))
    return jnp.concatenate([weights, weights]), own_index == owner_expiring


def phases(ordering):
    site = jnp.arange(K, dtype=jnp.int32)
    turn = (
        (site // LSIDE)[:, None] * (ordering // LSIDE)[None, :]
        + (site % LSIDE)[:, None] * (ordering % LSIDE)[None, :]
    ) % LSIDE
    angles = turn.astype(f32) * (2.0 * math.pi / LSIDE)
    return jnp.cos(angles) / LSIDE, jnp.sin(angles) / LSIDE


def product(left, right):
    return jnp.dot(left, right, precision=lax.Precision.HIGHEST, preferred_element_type=f32)


def contract(pattern, left, right):
    return jnp.einsum(
        pattern, left, right, precision=lax.Precision.HIGHEST, preferred_element_type=f32
    )


def rotated(joined):
    half = joined.shape[-1] // 2
    return jnp.concatenate([-joined[..., half:], joined[..., :half]], axis=-1)


def plain_sigma(joined, cos_table, sin_table, strength):
    layout, half = joined.shape, joined.shape[-1] // 2
    flat = joined.reshape(K, -1)
    with_cos = product(cos_table, flat).reshape(layout)
    with_sin = product(sin_table, flat).reshape(layout)
    c_re, c_im = with_cos[..., :half], with_cos[..., half:]
    s_re, s_im = with_sin[..., :half], with_sin[..., half:]
    site_re, site_im = c_re - s_im, c_im + s_re
    back_re, back_im = (c_re + s_im)[:, ::-1], (c_im - s_re)[:, ::-1]
    other_re, other_im = site_re[:, ::-1], site_im[:, ::-1]
    pair_re = site_re * other_re - site_im * other_im
    pair_im = site_re * other_im + site_im * other_re
    sig_re = -strength * (pair_re * back_re + pair_im * back_im)
    sig_im = -strength * (pair_im * back_re - pair_re * back_im)
    sig = jnp.concatenate([sig_re, sig_im], axis=-1).reshape(K, -1)
    back_cos = product(cos_table.T, sig).reshape(layout)
    back_sin = product(sin_table.T, sig).reshape(layout)
    out_re = back_cos[..., :half] + back_sin[..., half:]
    out_im = back_cos[..., half:] - back_sin[..., :half]
    return jnp.concatenate([out_re, out_im], axis=-1)


def plain_body(panel_start, block_guess, coupling, slab_owner, expiring, ordering):
    panel = panel_start.shape[2]
    weights, chosen = window_weights(
        slab_owner, expiring, lax.axis_index("tm"), lax.axis_size("tm"), panel
    )
    cos_table, sin_table = phases(ordering)
    strength = coupling[0] * coupling[0]
    step_scale = 1.0 / math.sqrt(panel)
    guess = lax.all_gather(block_guess, "tm", axis=2, tiled=True)
    current = panel_start
    for _ in range(PASSES):
        exchanged = lax.all_to_all(current, "mom", split_axis=2, concat_axis=0, tiled=True)
        sigma = plain_sigma(exchanged, cos_table, sin_table, strength)
        returned = lax.all_to_all(sigma, "mom", split_axis=0, concat_axis=2, tiled=True)
        stacked = jnp.concatenate([current, rotated(current)], axis=2)
        conv = lax.psum(-contract("ksau,ksbu->ksab", returned * weights, stacked), "tm")
        current = panel_start + step_scale * contract("ksab,ksbu->ksau", conv, stacked)
    stacked = jnp.concatenate([conv, rotated(conv)], axis=2)
    block = guess + step_scale * contract("ksab,ksbc->ksac", guess, stacked)
    return jnp.where(chosen, block, current)


def split(x):
    high = x.astype(bf16)
    return high, (x - high.astype(f32)).astype(bf16)


def dot(left, right, transposed=False):
    dims = (((1,), (1 if transposed else 0,)), ((), ()))
    return lax.dot_general(left, right, dims, preferred_element_type=f32)


def dot3(left, right, transposed=False):
    (lh, ll), (rh, rl) = left, right
    rows = lh.shape[0]
    both = dot(jnp.concatenate([lh, ll], axis=0), rh, transposed)
    return both[:rows] + (both[rows:] + dot(lh, rl, transposed))


def dot_spins(lefts, rights, transposed=False):
    rows = lefts[0].shape[0]
    left = []
    for x in lefts:
        high, low = split(x)
        left += [jnp.concatenate([high, high], axis=1), jnp.concatenate([low, jnp.zeros_like(low)], axis=1)]
    parts = [split(x) for x in rights]
    along, across = (1, 0) if transposed else (0, 1)
    right = jnp.concatenate([jnp.concatenate(p, axis=along) for p in parts], axis=across)
    out = dot(jnp.concatenate(left, axis=0), right, transposed)
    return [
        out[2 * i * rows : (2 * i + 1) * rows, i * LANES : (i + 1) * LANES]
        + out[(2 * i + 1) * rows : (2 * i + 2) * rows, i * LANES : (i + 1) * LANES]
        for i in range(2)
    ]


def first_half(shape):
    return lax.broadcasted_iota(jnp.int32, shape, 1) < LANES // 2


def swap(x):
    return pltpu.roll(x, LANES // 2, 1)


def stack_rotated(g):
    other = swap(g)
    return jnp.concatenate([g, jnp.where(first_half(g.shape), -other, other)], axis=0)


def site_kernel(pieces, count, strength_ref, weight_ref, fh_ref, fl_ref, bh_ref, bl_ref, x_ref, *refs):
    momenta, _, rows, _ = x_ref.shape
    x = x_ref.reshape(-1, LANES)
    outs = [y.reshape(-1, LANES) for y in refs[len(refs) - 1 - pieces : -1]]
    left = first_half((K, LANES))
    weight = weight_ref[...]
    scale = -strength_ref[0]

    def place(spin, row, momenta=momenta):
        return pl.ds(spin * rows + row, momenta, stride=2 * rows), slice(None)

    def put(spin, row, value):
        step = momenta // (pieces * count)
        for j, y in enumerate(outs):
            at = [(z * pieces + j) * step for z in range(count)]
            part = jnp.concatenate([value[i : i + step] for i in at], axis=0) if pieces > 1 else value
            y[place(spin, row, momenta // pieces)] = part

    @pl.loop(0, rows // 2)
    def _(pair):
        site = []
        for spin in range(2):
            a, b = x[place(spin, 2 * pair)], x[place(spin, 2 * pair + 1)]
            re = jnp.where(left, a, swap(b))
            im = jnp.where(left, swap(a), b)
            joined = split(jnp.concatenate([re, im], axis=1))
            out = dot3((fh_ref[...], fl_ref[...]), joined)
            c_re, c_im = out[:K, :LANES], out[:K, LANES:]
            s_re, s_im = out[K:, :LANES], out[K:, LANES:]
            site.append((c_re - s_im, c_im + s_re, c_re + s_im, c_im - s_re))
        (r0, i0, *_), (r1, i1, *_) = site
        pair_re = scale * (r0 * r1 - i0 * i1)
        pair_im = scale * (r0 * i1 + i0 * r1)
        for spin in range(2):
            _, _, m_re, m_im = site[1 - spin]
            sig_re = pair_re * m_re + pair_im * m_im
            sig_im = pair_im * m_re - pair_re * m_im
            joined = split(jnp.concatenate([sig_re, sig_im], axis=1))
            out = dot3((bh_ref[...], bl_ref[...]), joined)
            re = (out[:K, :LANES] + out[K:, LANES:]) * weight
            im = (out[:K, LANES:] - out[K:, :LANES]) * weight
            put(spin, 2 * pair, jnp.where(left, re, swap(im)))
            put(spin, 2 * pair + 1, jnp.where(left, swap(re), im))


def site_sigma(strength, weights, tables, x, count, pieces, after=()):
    vmem = pl.BlockSpec(memory_space=pltpu.VMEM)
    shape = (x.shape[0] // pieces, *x.shape[1:])
    return pl.pallas_call(
        functools.partial(site_kernel, pieces, count),
        out_shape=[pltpu.HBM(shape, f32)] * pieces + [MARK],
        in_specs=[pl.BlockSpec(memory_space=pltpu.SMEM)] + [vmem] * 6 + unread(after),
        out_specs=[vmem] * pieces + [MARK_SPEC],
        compiler_params=pltpu.CompilerParams(vmem_limit_bytes=VMEM_LIMIT),
        cost_estimate=SMALL,
        name="site_sigma",
    )(strength, weights, *tables, *held([x]), *after)


def cut_kernel(x_ref, y_ref):
    count, _, _, rows, _ = y_ref.shape
    for z in range(count):
        y_ref[z] = x_ref[:, :, z * rows : (z + 1) * rows, :]


def cut_rows(panel_start, chunk, total, count):
    momenta, spins = panel_start.shape[:2]
    step = momenta // 4
    return pl.pallas_call(
        cut_kernel,
        out_shape=pltpu.HBM((count, momenta, spins, total // count, LANES), f32),
        grid=(4,),
        in_specs=[pl.BlockSpec((step, spins, total, LANES), lambda i: (i, 0, chunk, 0))],
        out_specs=pl.BlockSpec((count, step, spins, total // count, LANES), lambda i: (0, i, 0, 0, 0)),
        compiler_params=pltpu.CompilerParams(vmem_limit_bytes=VMEM_LIMIT),
        cost_estimate=SMALL,
        name="cut_rows",
    )(*held([panel_start]))


def held(arrays):
    return [pltpu.with_memory_space_constraint(x, pltpu.HBM) for x in arrays]


def unread(after):
    return [pl.BlockSpec(memory_space=pl.ANY)] * len(after)


MARK = jax.ShapeDtypeStruct((8, LANES), f32)
MARK_SPEC = pl.BlockSpec(memory_space=pl.ANY)


def mark_of(x):
    return x[0, 0, :8]


def stacks(refs, k):
    return [stack_rotated(jnp.concatenate([x[k, spin] for x in refs], axis=0)) for spin in range(2)]


def conv_kernel(parts, info_ref, s_ref, *refs):
    g_refs, c_ref = refs[:parts], refs[-2]
    for k in range(c_ref.shape[0]):
        sigma = [jnp.concatenate([s_ref[z, k, spin] for z in range(s_ref.shape[0])], axis=0) for spin in range(2)]
        out = dot_spins(sigma, stacks(g_refs, k), transposed=True)
        for spin in range(2):
            c_ref[k, spin] = -out[spin]


def moved_by(info_ref_at=0):
    return lambda i, info: (info[info_ref_at] + i, 0, 0, 0)


def still(i, info):
    return (i, 0, 0, 0)


def cut_block(shape, at=0):
    return pl.BlockSpec((shape[0], KBLOCK, *shape[2:]), lambda i, info: (0, info[at] + i, 0, 0, 0))


def conv_rows(info, sigma, g_parts, kcount, whole, after=()):
    total = sigma.shape[0] * sigma.shape[3]
    return pl.pallas_call(
        functools.partial(conv_kernel, len(g_parts)),
        out_shape=[jax.ShapeDtypeStruct((kcount, 2, total, LANES), f32), MARK],
        grid_spec=pltpu.PrefetchScalarGridSpec(
            num_scalar_prefetch=1,
            grid=(kcount // KBLOCK,),
            in_specs=[cut_block(sigma.shape, 0 if whole else 4)]
            + [pl.BlockSpec((KBLOCK, *x.shape[1:]), moved_by()) for x in g_parts]
            + unread(after),
            out_specs=[pl.BlockSpec((KBLOCK, 2, total, LANES), still), MARK_SPEC],
        ),
        compiler_params=pltpu.CompilerParams(vmem_limit_bytes=VMEM_LIMIT),
        cost_estimate=SMALL,
        name="conv_rows",
    )(info, *held([sigma, *g_parts]), *after)


def update_kernel(outs, parts, step_scale, info_ref, mine_ref, other_ref, start_ref, *refs):
    g_refs, out_refs = refs[:parts], refs[len(refs) - 1 - outs : -1]
    now_ref, cut_refs = out_refs[0], out_refs[1:]
    own = pl.program_id(0) // (pl.num_programs(0) // 2) == info_ref[2]
    for k in range(now_ref.shape[0]):
        conv = [jnp.where(own, mine_ref[k, spin], other_ref[k, spin]) for spin in range(2)]
        moved = dot_spins(conv, stacks(g_refs, k))
        for spin in range(2):
            new = start_ref[k, spin] + step_scale * moved[spin]
            now_ref[k, spin] = new
            for cut in cut_refs:
                count, rows = cut.shape[0], cut.shape[3]
                for z in range(count):
                    cut[z, k, spin] = new[z * rows : (z + 1) * rows]


def update_rows(info, conv, panel_start, g_parts, chunk, count, step_scale, cuts, previous=(), after=()):
    momenta, spins, panel, _ = panel_start.shape
    part, _, total, _ = conv[0].shape
    block = WIDE * KBLOCK
    steps = part // block

    def of_piece(i, info):
        return (info[5] // WIDE + i, 0, 0, 0)

    shapes = [pltpu.HBM((momenta, spins, total, LANES), f32)]
    specs = [pl.BlockSpec((block, spins, total, LANES), of_piece)]
    if cuts:
        shape = (count, momenta, spins, total // count, LANES)
        shapes.append(pltpu.HBM(shape, f32))
        specs.append(pl.BlockSpec((count, block, *shape[2:]), lambda i, info: (0, info[5] // WIDE + i, 0, 0, 0)))
    first = 1 + 3 + len(g_parts)

    def half(side):
        return lambda i, info: (jnp.clip(i - steps * abs(side - info[2]), 0, steps - 1), 0, 0, 0)

    return pl.pallas_call(
        functools.partial(update_kernel, len(shapes), len(g_parts), step_scale),
        out_shape=shapes + [MARK],
        grid_spec=pltpu.PrefetchScalarGridSpec(
            num_scalar_prefetch=1,
            grid=(2 * steps,),
            in_specs=[
                pl.BlockSpec((block, spins, total, LANES), half(0)),
                pl.BlockSpec((block, spins, total, LANES), half(1)),
                pl.BlockSpec((block, spins, total, LANES), lambda i, info: (info[5] // WIDE + i, 0, chunk, 0)),
            ]
            + [pl.BlockSpec((block, *g.shape[1:]), of_piece) for g in g_parts]
            + unread(previous)
            + unread(after),
            out_specs=specs + [MARK_SPEC],
        ),
        input_output_aliases={first + i: i for i in range(len(previous))},
        compiler_params=pltpu.CompilerParams(vmem_limit_bytes=VMEM_LIMIT),
        cost_estimate=SMALL,
        name="update_rows",
    )(info, *conv, *held([panel_start, *g_parts]), *previous, *after)


def final_kernel(chunks, shares, piece, step_scale, info_ref, *refs):
    past = chunks - 1
    mine_refs, other_refs, c_ref, start_ref = refs[:past], refs[past : 2 * past], refs[2 * past], refs[2 * past + 1]
    refs = refs[2 * chunks :]
    now_refs, g_refs = refs[:past], refs[past : past + chunks]
    d_refs, out_ref = refs[past + chunks : past + chunks + shares], refs[-2]
    total = start_ref.shape[2]

    @pl.when(info_ref[3] == 0)
    def _():
        for k in range(out_ref.shape[0]):
            moved = dot_spins([c_ref[k, spin] for spin in range(2)], stacks(g_refs, k))
            for spin in range(2):
                for chunk, now in enumerate(now_refs):
                    out_ref[k, spin, pl.ds(chunk * total, total), :] = now[k, spin]
                out_ref[k, spin, pl.ds((chunks - 1) * total, total), :] = start_ref[k, spin] + step_scale * moved[spin]

    @pl.when(info_ref[3] == 1)
    def _():
        rows = d_refs[0].shape[2]
        for k in range(out_ref.shape[0]):
            guess = [jnp.concatenate([x[k, spin] for x in d_refs], axis=0) for spin in range(2)]
            own = info_ref[2] == piece
            past_c = [[jnp.where(own, m[k, spin], o[k, spin]) for m, o in zip(mine_refs, other_refs)] for spin in range(2)]
            conv = [jnp.concatenate([*past_c[spin], c_ref[k, spin]], axis=0) for spin in range(2)]
            moved = dot_spins(guess, [stack_rotated(c) for c in conv])
            for spin in range(2):
                block = guess[spin] + step_scale * moved[spin]
                for e in range(shares):
                    at = pl.ds(pl.multiple_of((info_ref[1] ^ e) * rows, rows), rows)
                    out_ref[k, spin, at, :] = block[e * rows : (e + 1) * rows]


def final_rows(info, piece, past, conv, panel_start, nows, g_parts, guess, step_scale, previous=(), after=()):
    momenta, spins, panel, _ = panel_start.shape
    chunks, total = len(past) + 1, conv.shape[2]
    picked = lambda i, info: (info[3] * (info[4] + i), 0, 0, 0)
    picked_moved = lambda i, info: (info[3] * (info[0] + i), 0, 0, 0)
    c_block = (KBLOCK, spins, total, LANES)
    first = 1 + 2 + 4 * (chunks - 1) + 1 + len(guess)
    return pl.pallas_call(
        functools.partial(final_kernel, chunks, len(guess), piece, step_scale),
        out_shape=[jax.ShapeDtypeStruct(panel_start.shape, f32), MARK],
        grid_spec=pltpu.PrefetchScalarGridSpec(
            num_scalar_prefetch=1,
            grid=(conv.shape[0] // KBLOCK,),
            in_specs=[pl.BlockSpec(c_block, picked)] * (2 * (chunks - 1))
            + [pl.BlockSpec(c_block, still)]
            + [pl.BlockSpec(c_block, lambda i, info: (info[0] + i, 0, chunks - 1, 0))]
            + [pl.BlockSpec(c_block, moved_by())] * (chunks - 1)
            + [pl.BlockSpec((KBLOCK, *g.shape[1:]), moved_by()) for g in g_parts]
            + [pl.BlockSpec((KBLOCK, *x.shape[1:]), picked_moved) for x in guess]
            + unread(previous)
            + unread(after),
            out_specs=[pl.BlockSpec((KBLOCK, spins, panel, LANES), moved_by()), MARK_SPEC],
        ),
        input_output_aliases={first + i: i for i in range(len(previous))},
        compiler_params=pltpu.CompilerParams(vmem_limit_bytes=VMEM_LIMIT),
        cost_estimate=SMALL,
        name="final_rows",
    )(info, *[m for m, _ in past], *[o for _, o in past], conv, *held([panel_start, *nows, *g_parts, *guess]), *previous, *after)


def add_kernel(a_ref, b_ref, *refs):
    refs[-2][...] = a_ref[...] + b_ref[...]


def added(a, b, after=()):
    vmem = pl.BlockSpec(memory_space=pltpu.VMEM)
    return pl.pallas_call(
        add_kernel,
        out_shape=[jax.ShapeDtypeStruct(a.shape, f32), MARK],
        in_specs=[vmem, vmem] + unread(after),
        out_specs=[vmem, MARK_SPEC],
        cost_estimate=SMALL,
        name="added",
    )(a, b, *after)


def pairs(size, d):
    return [(i, i ^ d) for i in range(size)]


def exchange(cut):
    return lax.all_to_all(cut, "mom", split_axis=0, concat_axis=0, tiled=True)


def table_parts(ordering):
    cos_table, sin_table = phases(ordering)
    out = []
    for table in (
        jnp.concatenate([cos_table, sin_table], axis=0),
        jnp.concatenate([cos_table.T, sin_table.T], axis=0),
    ):
        high = lax.reduce_precision(table, exponent_bits=8, mantissa_bits=7)
        out += [high.astype(bf16), (table - high).astype(bf16)]
    return out


def body(panel_start, block_guess, coupling, slab_owner, expiring, ordering):
    momenta, spins, panel, _ = panel_start.shape
    count, slabs = lax.axis_size("mom"), lax.axis_size("tm")
    my_tm = lax.axis_index("tm")
    weights, chosen = window_weights(slab_owner, expiring, my_tm, slabs, panel)
    weights = weights.reshape(1, LANES)
    strength = coupling * coupling
    step_scale = 1.0 / math.sqrt(panel)
    total = panel // CHUNKS
    rows = total // count
    core = my_tm % 2
    flag = chosen.astype(jnp.int32)

    def infos(pieces):
        piece = momenta // (KBLOCK * pieces)

        def info(j, side):
            own, at = side * (piece // 2), j * piece
            return jnp.stack([at + own, my_tm, core, flag, own, at]).astype(jnp.int32)

        return [(info(j, core), info(j, 1 - core)) for j in range(pieces)]

    infos_of = {1: infos(1), PIECES: infos(PIECES)}

    def gathered(x):
        out, gaps, bit = [x], [0], slabs // 2
        while bit:
            out += [lax.ppermute(y, "tm", pairs(slabs, bit)) for y in out]
            gaps += [g ^ bit for g in gaps]
            bit //= 2
        return [y for _, y in sorted(zip(gaps, out), key=lambda both: both[0])]

    def convolved(sigma, g_parts, pieces, j, after):
        whole, part = len(sigma) == 1, momenta // (2 * pieces)
        source, (own, other) = sigma[0 if whole else j], infos_of[pieces][j]
        taken, step = [], momenta // (2 * PIECES)
        for k in range(0, part, step):
            ahead = jnp.array([k, 0, 0, 0, k, 0], jnp.int32) // KBLOCK
            give, given = conv_rows(other + ahead, source, g_parts, step, whole, after)
            taken.append(lax.ppermute(give, "tm", pairs(slabs, 1)))
            after = (given,)
        keep, kept = conv_rows(own, source, g_parts, part, whole, after)
        mine = keep + (jnp.concatenate(taken, axis=0) if len(taken) > 1 else taken[0])
        before = (kept, mark_of(mine))
        bit = 2
        while 2 * bit < slabs:
            mine = mine + lax.ppermute(mine, "tm", pairs(slabs, bit))
            bit *= 2
        return (mine, lax.ppermute(mine, "tm", pairs(slabs, bit))), before

    def summed(two, after=()):
        mine, mark = added(*two, after) if after else (two[0] + two[1], None)
        return (mine, lax.ppermute(mine, "tm", pairs(slabs, 1))), (mark_of(mine) if mark is None else mark,)

    def updated(conv, g_parts, chunk, cuts, after=()):
        out = ()
        for j, halves in enumerate(conv):
            *out, mark = update_rows(
                infos_of[len(conv)][j][0], halves, panel_start, g_parts, chunk, count, step_scale, cuts, out, after
            )
            after = ()
        return out, (mark,)

    sent = [cut_rows(panel_start, c, total, count) for c in range(CHUNKS)]
    tables = table_parts(ordering)
    guess = gathered(block_guess)
    g_parts = [panel_start]
    before = tuple(mark_of(x) for x in guess)
    for sweep in range(PASSES):
        last = sweep == PASSES - 1
        arrived = [exchange(x) for x in sent]
        sigma = []
        for chunk in range(CHUNKS):
            site = arrived[chunk].reshape(K, spins, rows, LANES)
            cuts = PIECES if last and chunk == CHUNKS - 1 else 1
            *parts, mark = site_sigma(strength, weights, tables, site, count, cuts, before)
            before = (mark,)
            sigma.append([exchange(x.reshape(count, -1, spins, rows, LANES)) for x in parts])
        pending, news = [], []
        for chunk in range(CHUNKS - 1 if last else CHUNKS):
            pieces = 1 if last else PIECES
            twos = []
            for j in range(pieces):
                two, before = convolved(sigma[chunk], g_parts, pieces, j, before)
                twos.append(two)
            if last:
                pending.append(twos)
            else:
                sums = [summed(two) for two in twos]
                before = tuple(mark for _, marks in sums for mark in marks)
                new, before = updated([conv for conv, _ in sums], g_parts, chunk, True, before)
                news.append(new)
        if not last:
            g_parts = [n[0] for n in news]
            sent = [n[1] for n in news]

    def final_piece(j, conv, out, after):
        for which in range(2):
            *out, mark = final_rows(
                infos_of[PIECES][j][which], j, past, conv[which], panel_start, nows, g_parts, guess, step_scale, out, after
            )
            after = ()
        return out, (mark,)

    out, nows, past = (), [], []
    for j in range(PIECES):
        two, beside = convolved(sigma[-1], g_parts, PIECES, j, before)
        if j == 0:
            for c, twos in enumerate(pending):
                sums = [summed(two) for two in twos]
                new, beside = updated([conv for conv, _ in sums], g_parts, c, False, beside)
                nows.append(new[0])
                past.append(sums[0][0])
        else:
            out, beside = final_piece(j - 1, conv, out, beside)
        conv, before = summed(two, beside)
    return final_piece(PIECES - 1, conv, out, ())[0][0]


def fits(mesh):
    def tiled(panel_start, *_):
        momenta, spins, panel, width = panel_start.shape
        count, slabs = mesh.shape["mom"], mesh.shape["tm"]
        powers = all(n & (n - 1) == 0 for n in (count, slabs))
        local = momenta // count
        return (
            powers
            and slabs > 2
            and spins == 2 * mesh.shape["groups"]
            and width == LANES * slabs
            and 2 * panel == LANES
            and panel == CHUNKS * count * ROWS
            and local % (2 * PIECES * WIDE * KBLOCK) == 0
            and PIECES == 2
            and PASSES == 2
        )

    return tiled


def solution(mesh):
    def mapped(inner):
        return jax.shard_map(
            inner,
            mesh=mesh,
            in_specs=(
                P("mom", "groups", None, "tm"),
                P("mom", "groups", "tm", None),
                P("groups"),
                P("groups"),
                P("groups"),
                P(),
            ),
            out_specs=P("mom", "groups", None, "tm"),
            check_vma=False,
        )

    def chosen(*args):
        return mapped(body if fits(mesh)(*args) else plain_body)(*args)

    return chosen
```

```python
import functools
import math

import jax
import jax.numpy as jnp
from jax import lax
from jax.experimental import pallas as pl
from jax.experimental.pallas import tpu as pltpu
from jax.sharding import PartitionSpec as P

LSIDE = 16
K = 256
PASSES = 2
CHUNKS = 2
PIECES = 2
ROWS = 8
LANES = 128
KBLOCK = 8
WIDE = 2
VMEM_LIMIT = 16 * 2**20
f32, bf16 = jnp.float32, jnp.bfloat16
SMALL = pl.CostEstimate(flops=1, bytes_accessed=1, transcendentals=0)


def window_weights(slab_owner, expiring, own_index, slab_count, panel):
    blocks = jnp.arange(slab_count, dtype=jnp.int32)
    slab_mine = jnp.sum(blocks * (slab_owner == own_index).astype(jnp.int32))
    position = (slab_mine - expiring[0]) % slab_count
    window = slab_count * panel
    times = position * panel + jnp.arange(panel, dtype=jnp.int32)
    weights = jnp.exp(-1.5 * (window - 1 - times).astype(f32) / window) / math.sqrt(window)
    owner_expiring = jnp.sum(slab_owner * (blocks == expiring[0]).astype(jnp.int32))
    return jnp.concatenate([weights, weights]), own_index == owner_expiring


def phases(ordering):
    site = jnp.arange(K, dtype=jnp.int32)
    turn = (
        (site // LSIDE)[:, None] * (ordering // LSIDE)[None, :]
        + (site % LSIDE)[:, None] * (ordering % LSIDE)[None, :]
    ) % LSIDE
    angles = turn.astype(f32) * (2.0 * math.pi / LSIDE)
    return jnp.cos(angles) / LSIDE, jnp.sin(angles) / LSIDE


def product(left, right):
    return jnp.dot(left, right, precision=lax.Precision.HIGHEST, preferred_element_type=f32)


def contract(pattern, left, right):
    return jnp.einsum(
        pattern, left, right, precision=lax.Precision.HIGHEST, preferred_element_type=f32
    )


def rotated(joined):
    half = joined.shape[-1] // 2
    return jnp.concatenate([-joined[..., half:], joined[..., :half]], axis=-1)


def plain_sigma(joined, cos_table, sin_table, strength):
    layout, half = joined.shape, joined.shape[-1] // 2
    flat = joined.reshape(K, -1)
    with_cos = product(cos_table, flat).reshape(layout)
    with_sin = product(sin_table, flat).reshape(layout)
    c_re, c_im = with_cos[..., :half], with_cos[..., half:]
    s_re, s_im = with_sin[..., :half], with_sin[..., half:]
    site_re, site_im = c_re - s_im, c_im + s_re
    back_re, back_im = (c_re + s_im)[:, ::-1], (c_im - s_re)[:, ::-1]
    other_re, other_im = site_re[:, ::-1], site_im[:, ::-1]
    pair_re = site_re * other_re - site_im * other_im
    pair_im = site_re * other_im + site_im * other_re
    sig_re = -strength * (pair_re * back_re + pair_im * back_im)
    sig_im = -strength * (pair_im * back_re - pair_re * back_im)
    sig = jnp.concatenate([sig_re, sig_im], axis=-1).reshape(K, -1)
    back_cos = product(cos_table.T, sig).reshape(layout)
    back_sin = product(sin_table.T, sig).reshape(layout)
    out_re = back_cos[..., :half] + back_sin[..., half:]
    out_im = back_cos[..., half:] - back_sin[..., :half]
    return jnp.concatenate([out_re, out_im], axis=-1)


def plain_body(panel_start, block_guess, coupling, slab_owner, expiring, ordering):
    panel = panel_start.shape[2]
    weights, chosen = window_weights(
        slab_owner, expiring, lax.axis_index("tm"), lax.axis_size("tm"), panel
    )
    cos_table, sin_table = phases(ordering)
    strength = coupling[0] * coupling[0]
    step_scale = 1.0 / math.sqrt(panel)
    guess = lax.all_gather(block_guess, "tm", axis=2, tiled=True)
    current = panel_start
    for _ in range(PASSES):
        exchanged = lax.all_to_all(current, "mom", split_axis=2, concat_axis=0, tiled=True)
        sigma = plain_sigma(exchanged, cos_table, sin_table, strength)
        returned = lax.all_to_all(sigma, "mom", split_axis=0, concat_axis=2, tiled=True)
        stacked = jnp.concatenate([current, rotated(current)], axis=2)
        conv = lax.psum(-contract("ksau,ksbu->ksab", returned * weights, stacked), "tm")
        current = panel_start + step_scale * contract("ksab,ksbu->ksau", conv, stacked)
    stacked = jnp.concatenate([conv, rotated(conv)], axis=2)
    block = guess + step_scale * contract("ksab,ksbc->ksac", guess, stacked)
    return jnp.where(chosen, block, current)


def split(x):
    high = x.astype(bf16)
    return high, (x - high.astype(f32)).astype(bf16)


def dot(left, right, transposed=False):
    dims = (((1,), (1 if transposed else 0,)), ((), ()))
    return lax.dot_general(left, right, dims, preferred_element_type=f32)


def dot3(left, right, transposed=False):
    (lh, ll), (rh, rl) = left, right
    rows = lh.shape[0]
    both = dot(jnp.concatenate([lh, ll], axis=0), rh, transposed)
    return both[:rows] + (both[rows:] + dot(lh, rl, transposed))


def dot_spins(lefts, rights, transposed=False):
    rows = lefts[0].shape[0]
    left = []
    for x in lefts:
        high, low = split(x)
        left += [jnp.concatenate([high, high], axis=1), jnp.concatenate([low, jnp.zeros_like(low)], axis=1)]
    parts = [split(x) for x in rights]
    along, across = (1, 0) if transposed else (0, 1)
    right = jnp.concatenate([jnp.concatenate(p, axis=along) for p in parts], axis=across)
    out = dot(jnp.concatenate(left, axis=0), right, transposed)
    return [
        out[2 * i * rows : (2 * i + 1) * rows, i * LANES : (i + 1) * LANES]
        + out[(2 * i + 1) * rows : (2 * i + 2) * rows, i * LANES : (i + 1) * LANES]
        for i in range(2)
    ]


def first_half(shape):
    return lax.broadcasted_iota(jnp.int32, shape, 1) < LANES // 2


def swap(x):
    return pltpu.roll(x, LANES // 2, 1)


def stack_rotated(g):
    other = swap(g)
    return jnp.concatenate([g, jnp.where(first_half(g.shape), -other, other)], axis=0)


def site_kernel(pieces, count, strength_ref, weight_ref, fh_ref, fl_ref, bh_ref, bl_ref, x_ref, *refs):
    momenta, _, rows, _ = x_ref.shape
    x = x_ref.reshape(-1, LANES)
    outs = [y.reshape(-1, LANES) for y in refs[len(refs) - 1 - pieces : -1]]
    left = first_half((K, LANES))
    weight = weight_ref[...]
    scale = -strength_ref[0]

    def place(spin, row, momenta=momenta):
        return pl.ds(spin * rows + row, momenta, stride=2 * rows), slice(None)

    def put(spin, row, value):
        step = momenta // (pieces * count)
        for j, y in enumerate(outs):
            at = [(z * pieces + j) * step for z in range(count)]
            part = jnp.concatenate([value[i : i + step] for i in at], axis=0) if pieces > 1 else value
            y[place(spin, row, momenta // pieces)] = part

    @pl.loop(0, rows // 2)
    def _(pair):
        site = []
        for spin in range(2):
            a, b = x[place(spin, 2 * pair)], x[place(spin, 2 * pair + 1)]
            re = jnp.where(left, a, swap(b))
            im = jnp.where(left, swap(a), b)
            joined = split(jnp.concatenate([re, im], axis=1))
            out = dot3((fh_ref[...], fl_ref[...]), joined)
            c_re, c_im = out[:K, :LANES], out[:K, LANES:]
            s_re, s_im = out[K:, :LANES], out[K:, LANES:]
            site.append((c_re - s_im, c_im + s_re, c_re + s_im, c_im - s_re))
        (r0, i0, *_), (r1, i1, *_) = site
        pair_re = scale * (r0 * r1 - i0 * i1)
        pair_im = scale * (r0 * i1 + i0 * r1)
        for spin in range(2):
            _, _, m_re, m_im = site[1 - spin]
            sig_re = pair_re * m_re + pair_im * m_im
            sig_im = pair_im * m_re - pair_re * m_im
            joined = split(jnp.concatenate([sig_re, sig_im], axis=1))
            out = dot3((bh_ref[...], bl_ref[...]), joined)
            re = (out[:K, :LANES] + out[K:, LANES:]) * weight
            im = (out[:K, LANES:] - out[K:, :LANES]) * weight
            put(spin, 2 * pair, jnp.where(left, re, swap(im)))
            put(spin, 2 * pair + 1, jnp.where(left, swap(re), im))


def site_sigma(strength, weights, tables, x, count, pieces, after=()):
    vmem = pl.BlockSpec(memory_space=pltpu.VMEM)
    shape = (x.shape[0] // pieces, *x.shape[1:])
    return pl.pallas_call(
        functools.partial(site_kernel, pieces, count),
        out_shape=[pltpu.HBM(shape, f32)] * pieces + [MARK],
        in_specs=[pl.BlockSpec(memory_space=pltpu.SMEM)] + [vmem] * 6 + unread(after),
        out_specs=[vmem] * pieces + [MARK_SPEC],
        compiler_params=pltpu.CompilerParams(vmem_limit_bytes=VMEM_LIMIT),
        cost_estimate=SMALL,
        name="site_sigma",
    )(strength, weights, *tables, *held([x]), *after)


def cut_kernel(x_ref, y_ref):
    count, _, _, rows, _ = y_ref.shape
    for z in range(count):
        y_ref[z] = x_ref[:, :, z * rows : (z + 1) * rows, :]


def cut_rows(panel_start, chunk, total, count):
    momenta, spins = panel_start.shape[:2]
    step = momenta // 4
    return pl.pallas_call(
        cut_kernel,
        out_shape=pltpu.HBM((count, momenta, spins, total // count, LANES), f32),
        grid=(4,),
        in_specs=[pl.BlockSpec((step, spins, total, LANES), lambda i: (i, 0, chunk, 0))],
        out_specs=pl.BlockSpec((count, step, spins, total // count, LANES), lambda i: (0, i, 0, 0, 0)),
        compiler_params=pltpu.CompilerParams(vmem_limit_bytes=VMEM_LIMIT),
        cost_estimate=SMALL,
        name="cut_rows",
    )(*held([panel_start]))


def held(arrays):
    return [pltpu.with_memory_space_constraint(x, pltpu.HBM) for x in arrays]


def unread(after):
    return [pl.BlockSpec(memory_space=pl.ANY)] * len(after)


MARK = jax.ShapeDtypeStruct((8, LANES), f32)
MARK_SPEC = pl.BlockSpec(memory_space=pl.ANY)


def mark_of(x):
    return x[0, 0, :8]


def stacks(refs, k):
    return [stack_rotated(jnp.concatenate([x[k, spin] for x in refs], axis=0)) for spin in range(2)]


def conv_kernel(parts, info_ref, s_ref, *refs):
    g_refs, c_ref = refs[:parts], refs[-2]
    for k in range(c_ref.shape[0]):
        sigma = [jnp.concatenate([s_ref[z, k, spin] for z in range(s_ref.shape[0])], axis=0) for spin in range(2)]
        out = dot_spins(sigma, stacks(g_refs, k), transposed=True)
        for spin in range(2):
            c_ref[k, spin] = -out[spin]


def moved_by(info_ref_at=0):
    return lambda i, info: (info[info_ref_at] + i, 0, 0, 0)


def still(i, info):
    return (i, 0, 0, 0)


def cut_block(shape, at=0):
    return pl.BlockSpec((shape[0], KBLOCK, *shape[2:]), lambda i, info: (0, info[at] + i, 0, 0, 0))


def conv_rows(info, sigma, g_parts, kcount, whole, after=()):
    total = sigma.shape[0] * sigma.shape[3]
    return pl.pallas_call(
        functools.partial(conv_kernel, len(g_parts)),
        out_shape=[jax.ShapeDtypeStruct((kcount, 2, total, LANES), f32), MARK],
        grid_spec=pltpu.PrefetchScalarGridSpec(
            num_scalar_prefetch=1,
            grid=(kcount // KBLOCK,),
            in_specs=[cut_block(sigma.shape, 0 if whole else 4)]
            + [pl.BlockSpec((KBLOCK, *x.shape[1:]), moved_by()) for x in g_parts]
            + unread(after),
            out_specs=[pl.BlockSpec((KBLOCK, 2, total, LANES), still), MARK_SPEC],
        ),
        compiler_params=pltpu.CompilerParams(vmem_limit_bytes=VMEM_LIMIT),
        cost_estimate=SMALL,
        name="conv_rows",
    )(info, *held([sigma, *g_parts]), *after)


def update_kernel(outs, parts, step_scale, info_ref, mine_ref, other_ref, start_ref, *refs):
    g_refs, out_refs = refs[:parts], refs[len(refs) - 1 - outs : -1]
    now_ref, cut_refs = out_refs[0], out_refs[1:]
    own = pl.program_id(0) // (pl.num_programs(0) // 2) == info_ref[2]
    for k in range(now_ref.shape[0]):
        conv = [jnp.where(own, mine_ref[k, spin], other_ref[k, spin]) for spin in range(2)]
        moved = dot_spins(conv, stacks(g_refs, k))
        for spin in range(2):
            new = start_ref[k, spin] + step_scale * moved[spin]
            now_ref[k, spin] = new
            for cut in cut_refs:
                count, rows = cut.shape[0], cut.shape[3]
                for z in range(count):
                    cut[z, k, spin] = new[z * rows : (z + 1) * rows]


def update_rows(info, conv, panel_start, g_parts, chunk, count, step_scale, cuts, previous=(), after=()):
    momenta, spins, panel, _ = panel_start.shape
    part, _, total, _ = conv[0].shape
    block = WIDE * KBLOCK
    steps = part // block

    def of_piece(i, info):
        return (info[5] // WIDE + i, 0, 0, 0)

    shapes = [pltpu.HBM((momenta, spins, total, LANES), f32)]
    specs = [pl.BlockSpec((block, spins, total, LANES), of_piece)]
    if cuts:
        shape = (count, momenta, spins, total // count, LANES)
        shapes.append(pltpu.HBM(shape, f32))
        specs.append(pl.BlockSpec((count, block, *shape[2:]), lambda i, info: (0, info[5] // WIDE + i, 0, 0, 0)))
    first = 1 + 3 + len(g_parts)

    def half(side):
        return lambda i, info: (jnp.clip(i - steps * abs(side - info[2]), 0, steps - 1), 0, 0, 0)

    return pl.pallas_call(
        functools.partial(update_kernel, len(shapes), len(g_parts), step_scale),
        out_shape=shapes + [MARK],
        grid_spec=pltpu.PrefetchScalarGridSpec(
            num_scalar_prefetch=1,
            grid=(2 * steps,),
            in_specs=[
                pl.BlockSpec((block, spins, total, LANES), half(0)),
                pl.BlockSpec((block, spins, total, LANES), half(1)),
                pl.BlockSpec((block, spins, total, LANES), lambda i, info: (info[5] // WIDE + i, 0, chunk, 0)),
            ]
            + [pl.BlockSpec((block, *g.shape[1:]), of_piece) for g in g_parts]
            + unread(previous)
            + unread(after),
            out_specs=specs + [MARK_SPEC],
        ),
        input_output_aliases={first + i: i for i in range(len(previous))},
        compiler_params=pltpu.CompilerParams(vmem_limit_bytes=VMEM_LIMIT),
        cost_estimate=SMALL,
        name="update_rows",
    )(info, *conv, *held([panel_start, *g_parts]), *previous, *after)


def final_kernel(chunks, shares, piece, step_scale, info_ref, *refs):
    past = chunks - 1
    mine_refs, other_refs, c_ref, start_ref = refs[:past], refs[past : 2 * past], refs[2 * past], refs[2 * past + 1]
    refs = refs[2 * chunks :]
    now_refs, g_refs = refs[:past], refs[past : past + chunks]
    d_refs, out_ref = refs[past + chunks : past + chunks + shares], refs[-2]
    total = start_ref.shape[2]

    @pl.when(info_ref[3] == 0)
    def _():
        for k in range(out_ref.shape[0]):
            moved = dot_spins([c_ref[k, spin] for spin in range(2)], stacks(g_refs, k))
            for spin in range(2):
                for chunk, now in enumerate(now_refs):
                    out_ref[k, spin, pl.ds(chunk * total, total), :] = now[k, spin]
                out_ref[k, spin, pl.ds((chunks - 1) * total, total), :] = start_ref[k, spin] + step_scale * moved[spin]

    @pl.when(info_ref[3] == 1)
    def _():
        rows = d_refs[0].shape[2]
        for k in range(out_ref.shape[0]):
            guess = [jnp.concatenate([x[k, spin] for x in d_refs], axis=0) for spin in range(2)]
            own = info_ref[2] == piece
            past_c = [[jnp.where(own, m[k, spin], o[k, spin]) for m, o in zip(mine_refs, other_refs)] for spin in range(2)]
            conv = [jnp.concatenate([*past_c[spin], c_ref[k, spin]], axis=0) for spin in range(2)]
            moved = dot_spins(guess, [stack_rotated(c) for c in conv])
            for spin in range(2):
                block = guess[spin] + step_scale * moved[spin]
                for e in range(shares):
                    at = pl.ds(pl.multiple_of((info_ref[1] ^ e) * rows, rows), rows)
                    out_ref[k, spin, at, :] = block[e * rows : (e + 1) * rows]


def final_rows(info, piece, past, conv, panel_start, nows, g_parts, guess, step_scale, previous=(), after=()):
    momenta, spins, panel, _ = panel_start.shape
    chunks, total = len(past) + 1, conv.shape[2]
    picked = lambda i, info: (info[3] * (info[4] + i), 0, 0, 0)
    picked_moved = lambda i, info: (info[3] * (info[0] + i), 0, 0, 0)
    c_block = (KBLOCK, spins, total, LANES)
    first = 1 + 2 + 4 * (chunks - 1) + 1 + len(guess)
    return pl.pallas_call(
        functools.partial(final_kernel, chunks, len(guess), piece, step_scale),
        out_shape=[jax.ShapeDtypeStruct(panel_start.shape, f32), MARK],
        grid_spec=pltpu.PrefetchScalarGridSpec(
            num_scalar_prefetch=1,
            grid=(conv.shape[0] // KBLOCK,),
            in_specs=[pl.BlockSpec(c_block, picked)] * (2 * (chunks - 1))
            + [pl.BlockSpec(c_block, still)]
            + [pl.BlockSpec(c_block, lambda i, info: (info[0] + i, 0, chunks - 1, 0))]
            + [pl.BlockSpec(c_block, moved_by())] * (chunks - 1)
            + [pl.BlockSpec((KBLOCK, *g.shape[1:]), moved_by()) for g in g_parts]
            + [pl.BlockSpec((KBLOCK, *x.shape[1:]), picked_moved) for x in guess]
            + unread(previous)
            + unread(after),
            out_specs=[pl.BlockSpec((KBLOCK, spins, panel, LANES), moved_by()), MARK_SPEC],
        ),
        input_output_aliases={first + i: i for i in range(len(previous))},
        compiler_params=pltpu.CompilerParams(vmem_limit_bytes=VMEM_LIMIT),
        cost_estimate=SMALL,
        name="final_rows",
    )(info, *[m for m, _ in past], *[o for _, o in past], conv, *held([panel_start, *nows, *g_parts, *guess]), *previous, *after)


def add_kernel(a_ref, b_ref, *refs):
    refs[-2][...] = a_ref[...] + b_ref[...]


def added(a, b, after=()):
    vmem = pl.BlockSpec(memory_space=pltpu.VMEM)
    return pl.pallas_call(
        add_kernel,
        out_shape=[jax.ShapeDtypeStruct(a.shape, f32), MARK],
        in_specs=[vmem, vmem] + unread(after),
        out_specs=[vmem, MARK_SPEC],
        compiler_params=pltpu.CompilerParams(vmem_limit_bytes=VMEM_LIMIT // 4),
        cost_estimate=SMALL,
        name="added",
    )(a, b, *after)


def pairs(size, d):
    return [(i, i ^ d) for i in range(size)]


def exchange(cut):
    return lax.all_to_all(cut, "mom", split_axis=0, concat_axis=0, tiled=True)


def table_parts(ordering):
    cos_table, sin_table = phases(ordering)
    out = []
    for table in (
        jnp.concatenate([cos_table, sin_table], axis=0),
        jnp.concatenate([cos_table.T, sin_table.T], axis=0),
    ):
        high = lax.reduce_precision(table, exponent_bits=8, mantissa_bits=7)
        out += [high.astype(bf16), (table - high).astype(bf16)]
    return out


def body(panel_start, block_guess, coupling, slab_owner, expiring, ordering):
    momenta, spins, panel, _ = panel_start.shape
    count, slabs = lax.axis_size("mom"), lax.axis_size("tm")
    my_tm = lax.axis_index("tm")
    weights, chosen = window_weights(slab_owner, expiring, my_tm, slabs, panel)
    weights = weights.reshape(1, LANES)
    strength = coupling * coupling
    step_scale = 1.0 / math.sqrt(panel)
    total = panel // CHUNKS
    rows = total // count
    core = my_tm % 2
    flag = chosen.astype(jnp.int32)

    def infos(pieces):
        piece = momenta // (KBLOCK * pieces)

        def info(j, side):
            own, at = side * (piece // 2), j * piece
            return jnp.stack([at + own, my_tm, core, flag, own, at]).astype(jnp.int32)

        return [(info(j, core), info(j, 1 - core)) for j in range(pieces)]

    infos_of = {1: infos(1), PIECES: infos(PIECES)}

    def gathered(x):
        out, gaps, bit = [x], [0], slabs // 2
        while bit:
            out += [lax.ppermute(y, "tm", pairs(slabs, bit)) for y in out]
            gaps += [g ^ bit for g in gaps]
            bit //= 2
        return [y for _, y in sorted(zip(gaps, out), key=lambda both: both[0])]

    def convolved(sigma, g_parts, pieces, j, after):
        whole, part = len(sigma) == 1, momenta // (2 * pieces)
        source, (own, other) = sigma[0 if whole else j], infos_of[pieces][j]
        taken, step = [], momenta // (2 * PIECES)
        for k in range(0, part, step):
            ahead = jnp.array([k, 0, 0, 0, k, 0], jnp.int32) // KBLOCK
            give, given = conv_rows(other + ahead, source, g_parts, step, whole, after)
            taken.append(lax.ppermute(give, "tm", pairs(slabs, 1)))
            after = (given,)
        keep, kept = conv_rows(own, source, g_parts, part, whole, after)
        mine = keep + (jnp.concatenate(taken, axis=0) if len(taken) > 1 else taken[0])
        before = (kept, mark_of(mine))
        bit = 2
        while 2 * bit < slabs:
            mine = mine + lax.ppermute(mine, "tm", pairs(slabs, bit))
            bit *= 2
        return (mine, lax.ppermute(mine, "tm", pairs(slabs, bit))), before

    def summed(two, after=()):
        mine, mark = added(*two, after) if after else (two[0] + two[1], None)
        return (mine, lax.ppermute(mine, "tm", pairs(slabs, 1))), (mark_of(mine) if mark is None else mark,)

    def updated(conv, g_parts, chunk, cuts, after=()):
        out = ()
        for j, halves in enumerate(conv):
            *out, mark = update_rows(
                infos_of[len(conv)][j][0], halves, panel_start, g_parts, chunk, count, step_scale, cuts, out, after
            )
            after = ()
        return out, (mark,)

    sent = [cut_rows(panel_start, c, total, count) for c in range(CHUNKS)]
    tables = table_parts(ordering)
    guess = gathered(block_guess)
    g_parts = [panel_start]
    before = tuple(mark_of(x) for x in guess)
    for sweep in range(PASSES):
        last = sweep == PASSES - 1
        arrived = [exchange(x) for x in sent]
        sigma = []
        for chunk in range(CHUNKS):
            site = arrived[chunk].reshape(K, spins, rows, LANES)
            cuts = PIECES if last and chunk == CHUNKS - 1 else 1
            *parts, mark = site_sigma(strength, weights, tables, site, count, cuts, before)
            before = (mark,)
            sigma.append([exchange(x.reshape(count, -1, spins, rows, LANES)) for x in parts])
        pending, news = [], []
        for chunk in range(CHUNKS - 1 if last else CHUNKS):
            pieces = 1 if last else PIECES
            twos = []
            for j in range(pieces):
                two, before = convolved(sigma[chunk], g_parts, pieces, j, before)
                twos.append(two)
            if last:
                pending.append(twos)
            else:
                sums = [summed(two) for two in twos]
                before = tuple(mark for _, marks in sums for mark in marks)
                new, before = updated([conv for conv, _ in sums], g_parts, chunk, True, before)
                news.append(new)
        if not last:
            g_parts = [n[0] for n in news]
            sent = [n[1] for n in news]

    def final_piece(j, conv, out, after):
        for which in range(2):
            *out, mark = final_rows(
                infos_of[PIECES][j][which], j, past, conv[which], panel_start, nows, g_parts, guess, step_scale, out, after
            )
            after = ()
        return out, (mark,)

    out, nows, past = (), [], []
    for j in range(PIECES):
        two, beside = convolved(sigma[-1], g_parts, PIECES, j, before)
        if j == 0:
            for c, twos in enumerate(pending):
                sums = [summed(two) for two in twos]
                new, beside = updated([conv for conv, _ in sums], g_parts, c, False, beside)
                nows.append(new[0])
                past.append(sums[0][0])
        else:
            out, beside = final_piece(j - 1, conv, out, beside)
        conv, before = summed(two, beside)
    return final_piece(PIECES - 1, conv, out, ())[0][0]


def fits(mesh):
    def tiled(panel_start, *_):
        momenta, spins, panel, width = panel_start.shape
        count, slabs = mesh.shape["mom"], mesh.shape["tm"]
        powers = all(n & (n - 1) == 0 for n in (count, slabs))
        local = momenta // count
        return (
            powers
            and slabs > 2
            and spins == 2 * mesh.shape["groups"]
            and width == LANES * slabs
            and 2 * panel == LANES
            and panel == CHUNKS * count * ROWS
            and local % (2 * PIECES * WIDE * KBLOCK) == 0
            and PIECES == 2
            and PASSES == 2
        )

    return tiled


def solution(mesh):
    def mapped(inner):
        return jax.shard_map(
            inner,
            mesh=mesh,
            in_specs=(
                P("mom", "groups", None, "tm"),
                P("mom", "groups", "tm", None),
                P("groups"),
                P("groups"),
                P("groups"),
                P(),
            ),
            out_specs=P("mom", "groups", None, "tm"),
            check_vma=False,
        )

    def chosen(*args):
        return mapped(body if fits(mesh)(*args) else plain_body)(*args)

    return chosen
```

```python
import functools
import math

import jax
import jax.numpy as jnp
from jax import lax
from jax.experimental import pallas as pl
from jax.experimental.pallas import tpu as pltpu
from jax.sharding import PartitionSpec as P

LSIDE = 16
K = 256
PASSES = 2
CHUNKS = 2
PIECES = 2
ROWS = 8
LANES = 128
KBLOCK = 8
WIDE = 2
VMEM_LIMIT = 12 * 2**20
f32, bf16 = jnp.float32, jnp.bfloat16
SMALL = pl.CostEstimate(flops=1, bytes_accessed=1, transcendentals=0)


def window_weights(slab_owner, expiring, own_index, slab_count, panel):
    blocks = jnp.arange(slab_count, dtype=jnp.int32)
    slab_mine = jnp.sum(blocks * (slab_owner == own_index).astype(jnp.int32))
    position = (slab_mine - expiring[0]) % slab_count
    window = slab_count * panel
    times = position * panel + jnp.arange(panel, dtype=jnp.int32)
    weights = jnp.exp(-1.5 * (window - 1 - times).astype(f32) / window) / math.sqrt(window)
    owner_expiring = jnp.sum(slab_owner * (blocks == expiring[0]).astype(jnp.int32))
    return jnp.concatenate([weights, weights]), own_index == owner_expiring


def phases(ordering):
    site = jnp.arange(K, dtype=jnp.int32)
    turn = (
        (site // LSIDE)[:, None] * (ordering // LSIDE)[None, :]
        + (site % LSIDE)[:, None] * (ordering % LSIDE)[None, :]
    ) % LSIDE
    angles = turn.astype(f32) * (2.0 * math.pi / LSIDE)
    return jnp.cos(angles) / LSIDE, jnp.sin(angles) / LSIDE


def product(left, right):
    return jnp.dot(left, right, precision=lax.Precision.HIGHEST, preferred_element_type=f32)


def contract(pattern, left, right):
    return jnp.einsum(
        pattern, left, right, precision=lax.Precision.HIGHEST, preferred_element_type=f32
    )


def rotated(joined):
    half = joined.shape[-1] // 2
    return jnp.concatenate([-joined[..., half:], joined[..., :half]], axis=-1)


def plain_sigma(joined, cos_table, sin_table, strength):
    layout, half = joined.shape, joined.shape[-1] // 2
    flat = joined.reshape(K, -1)
    with_cos = product(cos_table, flat).reshape(layout)
    with_sin = product(sin_table, flat).reshape(layout)
    c_re, c_im = with_cos[..., :half], with_cos[..., half:]
    s_re, s_im = with_sin[..., :half], with_sin[..., half:]
    site_re, site_im = c_re - s_im, c_im + s_re
    back_re, back_im = (c_re + s_im)[:, ::-1], (c_im - s_re)[:, ::-1]
    other_re, other_im = site_re[:, ::-1], site_im[:, ::-1]
    pair_re = site_re * other_re - site_im * other_im
    pair_im = site_re * other_im + site_im * other_re
    sig_re = -strength * (pair_re * back_re + pair_im * back_im)
    sig_im = -strength * (pair_im * back_re - pair_re * back_im)
    sig = jnp.concatenate([sig_re, sig_im], axis=-1).reshape(K, -1)
    back_cos = product(cos_table.T, sig).reshape(layout)
    back_sin = product(sin_table.T, sig).reshape(layout)
    out_re = back_cos[..., :half] + back_sin[..., half:]
    out_im = back_cos[..., half:] - back_sin[..., :half]
    return jnp.concatenate([out_re, out_im], axis=-1)


def plain_body(panel_start, block_guess, coupling, slab_owner, expiring, ordering):
    panel = panel_start.shape[2]
    weights, chosen = window_weights(
        slab_owner, expiring, lax.axis_index("tm"), lax.axis_size("tm"), panel
    )
    cos_table, sin_table = phases(ordering)
    strength = coupling[0] * coupling[0]
    step_scale = 1.0 / math.sqrt(panel)
    guess = lax.all_gather(block_guess, "tm", axis=2, tiled=True)
    current = panel_start
    for _ in range(PASSES):
        exchanged = lax.all_to_all(current, "mom", split_axis=2, concat_axis=0, tiled=True)
        sigma = plain_sigma(exchanged, cos_table, sin_table, strength)
        returned = lax.all_to_all(sigma, "mom", split_axis=0, concat_axis=2, tiled=True)
        stacked = jnp.concatenate([current, rotated(current)], axis=2)
        conv = lax.psum(-contract("ksau,ksbu->ksab", returned * weights, stacked), "tm")
        current = panel_start + step_scale * contract("ksab,ksbu->ksau", conv, stacked)
    stacked = jnp.concatenate([conv, rotated(conv)], axis=2)
    block = guess + step_scale * contract("ksab,ksbc->ksac", guess, stacked)
    return jnp.where(chosen, block, current)


def split(x):
    high = x.astype(bf16)
    return high, (x - high.astype(f32)).astype(bf16)


def dot(left, right, transposed=False):
    dims = (((1,), (1 if transposed else 0,)), ((), ()))
    return lax.dot_general(left, right, dims, preferred_element_type=f32)


def dot3(left, right, transposed=False):
    (lh, ll), (rh, rl) = left, right
    rows = lh.shape[0]
    both = dot(jnp.concatenate([lh, ll], axis=0), rh, transposed)
    return both[:rows] + (both[rows:] + dot(lh, rl, transposed))


def dot_spins(lefts, rights, transposed=False):
    rows = lefts[0].shape[0]
    left = []
    for x in lefts:
        high, low = split(x)
        left += [jnp.concatenate([high, high], axis=1), jnp.concatenate([low, jnp.zeros_like(low)], axis=1)]
    parts = [split(x) for x in rights]
    along, across = (1, 0) if transposed else (0, 1)
    right = jnp.concatenate([jnp.concatenate(p, axis=along) for p in parts], axis=across)
    out = dot(jnp.concatenate(left, axis=0), right, transposed)
    return [
        out[2 * i * rows : (2 * i + 1) * rows, i * LANES : (i + 1) * LANES]
        + out[(2 * i + 1) * rows : (2 * i + 2) * rows, i * LANES : (i + 1) * LANES]
        for i in range(2)
    ]


def first_half(shape):
    return lax.broadcasted_iota(jnp.int32, shape, 1) < LANES // 2


def swap(x):
    return pltpu.roll(x, LANES // 2, 1)


def stack_rotated(g):
    other = swap(g)
    return jnp.concatenate([g, jnp.where(first_half(g.shape), -other, other)], axis=0)


def site_kernel(pieces, count, strength_ref, weight_ref, fh_ref, fl_ref, bh_ref, bl_ref, x_ref, *refs):
    momenta, _, rows, _ = x_ref.shape
    x = x_ref.reshape(-1, LANES)
    outs = [y.reshape(-1, LANES) for y in refs[len(refs) - 1 - pieces : -1]]
    left = first_half((K, LANES))
    weight = weight_ref[...]
    scale = -strength_ref[0]

    def place(spin, row, momenta=momenta):
        return pl.ds(spin * rows + row, momenta, stride=2 * rows), slice(None)

    def put(spin, row, value):
        step = momenta // (pieces * count)
        for j, y in enumerate(outs):
            at = [(z * pieces + j) * step for z in range(count)]
            part = jnp.concatenate([value[i : i + step] for i in at], axis=0) if pieces > 1 else value
            y[place(spin, row, momenta // pieces)] = part

    @pl.loop(0, rows // 2)
    def _(pair):
        site = []
        for spin in range(2):
            a, b = x[place(spin, 2 * pair)], x[place(spin, 2 * pair + 1)]
            re = jnp.where(left, a, swap(b))
            im = jnp.where(left, swap(a), b)
            joined = split(jnp.concatenate([re, im], axis=1))
            out = dot3((fh_ref[...], fl_ref[...]), joined)
            c_re, c_im = out[:K, :LANES], out[:K, LANES:]
            s_re, s_im = out[K:, :LANES], out[K:, LANES:]
            site.append((c_re - s_im, c_im + s_re, c_re + s_im, c_im - s_re))
        (r0, i0, *_), (r1, i1, *_) = site
        pair_re = scale * (r0 * r1 - i0 * i1)
        pair_im = scale * (r0 * i1 + i0 * r1)
        for spin in range(2):
            _, _, m_re, m_im = site[1 - spin]
            sig_re = pair_re * m_re + pair_im * m_im
            sig_im = pair_im * m_re - pair_re * m_im
            joined = split(jnp.concatenate([sig_re, sig_im], axis=1))
            out = dot3((bh_ref[...], bl_ref[...]), joined)
            re = (out[:K, :LANES] + out[K:, LANES:]) * weight
            im = (out[:K, LANES:] - out[K:, :LANES]) * weight
            put(spin, 2 * pair, jnp.where(left, re, swap(im)))
            put(spin, 2 * pair + 1, jnp.where(left, swap(re), im))


def site_sigma(strength, weights, tables, x, count, pieces, after=()):
    vmem = pl.BlockSpec(memory_space=pltpu.VMEM)
    shape = (x.shape[0] // pieces, *x.shape[1:])
    return pl.pallas_call(
        functools.partial(site_kernel, pieces, count),
        out_shape=[pltpu.HBM(shape, f32)] * pieces + [MARK],
        in_specs=[pl.BlockSpec(memory_space=pltpu.SMEM)] + [vmem] * 6 + unread(after),
        out_specs=[vmem] * pieces + [MARK_SPEC],
        compiler_params=pltpu.CompilerParams(vmem_limit_bytes=VMEM_LIMIT),
        cost_estimate=SMALL,
        name="site_sigma",
    )(strength, weights, *tables, *held([x]), *after)


def cut_kernel(x_ref, y_ref):
    count, _, _, rows, _ = y_ref.shape
    for z in range(count):
        y_ref[z] = x_ref[:, :, z * rows : (z + 1) * rows, :]


def cut_rows(panel_start, chunk, total, count):
    momenta, spins = panel_start.shape[:2]
    step = momenta // 4
    return pl.pallas_call(
        cut_kernel,
        out_shape=pltpu.HBM((count, momenta, spins, total // count, LANES), f32),
        grid=(4,),
        in_specs=[pl.BlockSpec((step, spins, total, LANES), lambda i: (i, 0, chunk, 0))],
        out_specs=pl.BlockSpec((count, step, spins, total // count, LANES), lambda i: (0, i, 0, 0, 0)),
        compiler_params=pltpu.CompilerParams(vmem_limit_bytes=VMEM_LIMIT),
        cost_estimate=SMALL,
        name="cut_rows",
    )(*held([panel_start]))


def held(arrays):
    return [pltpu.with_memory_space_constraint(x, pltpu.HBM) for x in arrays]


def unread(after):
    return [pl.BlockSpec(memory_space=pl.ANY)] * len(after)


MARK = jax.ShapeDtypeStruct((8, LANES), f32)
MARK_SPEC = pl.BlockSpec(memory_space=pl.ANY)


def mark_of(x):
    return x[0, 0, :8]


def stacks(refs, k):
    return [stack_rotated(jnp.concatenate([x[k, spin] for x in refs], axis=0)) for spin in range(2)]


def conv_kernel(parts, info_ref, s_ref, *refs):
    g_refs, c_ref = refs[:parts], refs[-2]
    for k in range(c_ref.shape[0]):
        sigma = [jnp.concatenate([s_ref[z, k, spin] for z in range(s_ref.shape[0])], axis=0) for spin in range(2)]
        out = dot_spins(sigma, stacks(g_refs, k), transposed=True)
        for spin in range(2):
            c_ref[k, spin] = -out[spin]


def moved_by(info_ref_at=0):
    return lambda i, info: (info[info_ref_at] + i, 0, 0, 0)


def still(i, info):
    return (i, 0, 0, 0)


def cut_block(shape, at=0):
    return pl.BlockSpec((shape[0], KBLOCK, *shape[2:]), lambda i, info: (0, info[at] + i, 0, 0, 0))


def conv_rows(info, sigma, g_parts, kcount, whole, after=()):
    total = sigma.shape[0] * sigma.shape[3]
    return pl.pallas_call(
        functools.partial(conv_kernel, len(g_parts)),
        out_shape=[jax.ShapeDtypeStruct((kcount, 2, total, LANES), f32), MARK],
        grid_spec=pltpu.PrefetchScalarGridSpec(
            num_scalar_prefetch=1,
            grid=(kcount // KBLOCK,),
            in_specs=[cut_block(sigma.shape, 0 if whole else 4)]
            + [pl.BlockSpec((KBLOCK, *x.shape[1:]), moved_by()) for x in g_parts]
            + unread(after),
            out_specs=[pl.BlockSpec((KBLOCK, 2, total, LANES), still), MARK_SPEC],
        ),
        compiler_params=pltpu.CompilerParams(vmem_limit_bytes=VMEM_LIMIT),
        cost_estimate=SMALL,
        name="conv_rows",
    )(info, *held([sigma, *g_parts]), *after)


def update_kernel(outs, parts, step_scale, info_ref, mine_ref, other_ref, start_ref, *refs):
    g_refs, out_refs = refs[:parts], refs[len(refs) - 1 - outs : -1]
    now_ref, cut_refs = out_refs[0], out_refs[1:]
    own = pl.program_id(0) // (pl.num_programs(0) // 2) == info_ref[2]
    for k in range(now_ref.shape[0]):
        conv = [jnp.where(own, mine_ref[k, spin], other_ref[k, spin]) for spin in range(2)]
        moved = dot_spins(conv, stacks(g_refs, k))
        for spin in range(2):
            new = start_ref[k, spin] + step_scale * moved[spin]
            now_ref[k, spin] = new
            for cut in cut_refs:
                count, rows = cut.shape[0], cut.shape[3]
                for z in range(count):
                    cut[z, k, spin] = new[z * rows : (z + 1) * rows]


def update_rows(info, conv, panel_start, g_parts, chunk, count, step_scale, cuts, previous=(), after=()):
    momenta, spins, panel, _ = panel_start.shape
    part, _, total, _ = conv[0].shape
    block = WIDE * KBLOCK
    steps = part // block

    def of_piece(i, info):
        return (info[5] // WIDE + i, 0, 0, 0)

    shapes = [pltpu.HBM((momenta, spins, total, LANES), f32)]
    specs = [pl.BlockSpec((block, spins, total, LANES), of_piece)]
    if cuts:
        shape = (count, momenta, spins, total // count, LANES)
        shapes.append(pltpu.HBM(shape, f32))
        specs.append(pl.BlockSpec((count, block, *shape[2:]), lambda i, info: (0, info[5] // WIDE + i, 0, 0, 0)))
    first = 1 + 3 + len(g_parts)

    def half(side):
        return lambda i, info: (jnp.clip(i - steps * abs(side - info[2]), 0, steps - 1), 0, 0, 0)

    return pl.pallas_call(
        functools.partial(update_kernel, len(shapes), len(g_parts), step_scale),
        out_shape=shapes + [MARK],
        grid_spec=pltpu.PrefetchScalarGridSpec(
            num_scalar_prefetch=1,
            grid=(2 * steps,),
            in_specs=[
                pl.BlockSpec((block, spins, total, LANES), half(0)),
                pl.BlockSpec((block, spins, total, LANES), half(1)),
                pl.BlockSpec((block, spins, total, LANES), lambda i, info: (info[5] // WIDE + i, 0, chunk, 0)),
            ]
            + [pl.BlockSpec((block, *g.shape[1:]), of_piece) for g in g_parts]
            + unread(previous)
            + unread(after),
            out_specs=specs + [MARK_SPEC],
        ),
        input_output_aliases={first + i: i for i in range(len(previous))},
        compiler_params=pltpu.CompilerParams(vmem_limit_bytes=VMEM_LIMIT),
        cost_estimate=SMALL,
        name="update_rows",
    )(info, *conv, *held([panel_start, *g_parts]), *previous, *after)


def final_kernel(chunks, shares, piece, step_scale, info_ref, *refs):
    past = chunks - 1
    mine_refs, other_refs, c_ref, start_ref = refs[:past], refs[past : 2 * past], refs[2 * past], refs[2 * past + 1]
    refs = refs[2 * chunks :]
    now_refs, g_refs = refs[:past], refs[past : past + chunks]
    d_refs, out_ref = refs[past + chunks : past + chunks + shares], refs[-2]
    total = start_ref.shape[2]

    @pl.when(info_ref[3] == 0)
    def _():
        for k in range(out_ref.shape[0]):
            moved = dot_spins([c_ref[k, spin] for spin in range(2)], stacks(g_refs, k))
            for spin in range(2):
                for chunk, now in enumerate(now_refs):
                    out_ref[k, spin, pl.ds(chunk * total, total), :] = now[k, spin]
                out_ref[k, spin, pl.ds((chunks - 1) * total, total), :] = start_ref[k, spin] + step_scale * moved[spin]

    @pl.when(info_ref[3] == 1)
    def _():
        rows = d_refs[0].shape[2]
        for k in range(out_ref.shape[0]):
            guess = [jnp.concatenate([x[k, spin] for x in d_refs], axis=0) for spin in range(2)]
            own = info_ref[2] == piece
            past_c = [[jnp.where(own, m[k, spin], o[k, spin]) for m, o in zip(mine_refs, other_refs)] for spin in range(2)]
            conv = [jnp.concatenate([*past_c[spin], c_ref[k, spin]], axis=0) for spin in range(2)]
            moved = dot_spins(guess, [stack_rotated(c) for c in conv])
            for spin in range(2):
                block = guess[spin] + step_scale * moved[spin]
                for e in range(shares):
                    at = pl.ds(pl.multiple_of((info_ref[1] ^ e) * rows, rows), rows)
                    out_ref[k, spin, at, :] = block[e * rows : (e + 1) * rows]


def final_rows(info, piece, past, conv, panel_start, nows, g_parts, guess, step_scale, previous=(), after=()):
    momenta, spins, panel, _ = panel_start.shape
    chunks, total = len(past) + 1, conv.shape[2]
    picked = lambda i, info: (info[3] * (info[4] + i), 0, 0, 0)
    picked_moved = lambda i, info: (info[3] * (info[0] + i), 0, 0, 0)
    c_block = (KBLOCK, spins, total, LANES)
    first = 1 + 2 + 4 * (chunks - 1) + 1 + len(guess)
    return pl.pallas_call(
        functools.partial(final_kernel, chunks, len(guess), piece, step_scale),
        out_shape=[jax.ShapeDtypeStruct(panel_start.shape, f32), MARK],
        grid_spec=pltpu.PrefetchScalarGridSpec(
            num_scalar_prefetch=1,
            grid=(conv.shape[0] // KBLOCK,),
            in_specs=[pl.BlockSpec(c_block, picked)] * (2 * (chunks - 1))
            + [pl.BlockSpec(c_block, still)]
            + [pl.BlockSpec(c_block, lambda i, info: (info[0] + i, 0, chunks - 1, 0))]
            + [pl.BlockSpec(c_block, moved_by())] * (chunks - 1)
            + [pl.BlockSpec((KBLOCK, *g.shape[1:]), moved_by()) for g in g_parts]
            + [pl.BlockSpec((KBLOCK, *x.shape[1:]), picked_moved) for x in guess]
            + unread(previous)
            + unread(after),
            out_specs=[pl.BlockSpec((KBLOCK, spins, panel, LANES), moved_by()), MARK_SPEC],
        ),
        input_output_aliases={first + i: i for i in range(len(previous))},
        compiler_params=pltpu.CompilerParams(vmem_limit_bytes=VMEM_LIMIT),
        cost_estimate=SMALL,
        name="final_rows",
    )(info, *[m for m, _ in past], *[o for _, o in past], conv, *held([panel_start, *nows, *g_parts, *guess]), *previous, *after)


def add_kernel(a_ref, b_ref, *refs):
    refs[-2][...] = a_ref[...] + b_ref[...]


def added(a, b, after=()):
    vmem = pl.BlockSpec(memory_space=pltpu.VMEM)
    return pl.pallas_call(
        add_kernel,
        out_shape=[jax.ShapeDtypeStruct(a.shape, f32), MARK],
        in_specs=[vmem, vmem] + unread(after),
        out_specs=[vmem, MARK_SPEC],
        compiler_params=pltpu.CompilerParams(vmem_limit_bytes=VMEM_LIMIT // 4),
        cost_estimate=SMALL,
        name="added",
    )(a, b, *after)


def pairs(size, d):
    return [(i, i ^ d) for i in range(size)]


def exchange(cut):
    return lax.all_to_all(cut, "mom", split_axis=0, concat_axis=0, tiled=True)


def table_parts(ordering):
    cos_table, sin_table = phases(ordering)
    out = []
    for table in (
        jnp.concatenate([cos_table, sin_table], axis=0),
        jnp.concatenate([cos_table.T, sin_table.T], axis=0),
    ):
        high = lax.reduce_precision(table, exponent_bits=8, mantissa_bits=7)
        out += [high.astype(bf16), (table - high).astype(bf16)]
    return out


def body(panel_start, block_guess, coupling, slab_owner, expiring, ordering):
    momenta, spins, panel, _ = panel_start.shape
    count, slabs = lax.axis_size("mom"), lax.axis_size("tm")
    my_tm = lax.axis_index("tm")
    weights, chosen = window_weights(slab_owner, expiring, my_tm, slabs, panel)
    weights = weights.reshape(1, LANES)
    strength = coupling * coupling
    step_scale = 1.0 / math.sqrt(panel)
    total = panel // CHUNKS
    rows = total // count
    core = my_tm % 2
    flag = chosen.astype(jnp.int32)

    def infos(pieces):
        piece = momenta // (KBLOCK * pieces)

        def info(j, side):
            own, at = side * (piece // 2), j * piece
            return jnp.stack([at + own, my_tm, core, flag, own, at]).astype(jnp.int32)

        return [(info(j, core), info(j, 1 - core)) for j in range(pieces)]

    infos_of = {1: infos(1), PIECES: infos(PIECES)}

    def gathered(x):
        out, gaps, bit = [x], [0], slabs // 2
        while bit:
            out += [lax.ppermute(y, "tm", pairs(slabs, bit)) for y in out]
            gaps += [g ^ bit for g in gaps]
            bit //= 2
        return [y for _, y in sorted(zip(gaps, out), key=lambda both: both[0])]

    def convolved(sigma, g_parts, pieces, j, after):
        whole, part = len(sigma) == 1, momenta // (2 * pieces)
        source, (own, other) = sigma[0 if whole else j], infos_of[pieces][j]
        taken, step = [], momenta // (2 * PIECES)
        for k in range(0, part, step):
            ahead = jnp.array([k, 0, 0, 0, k, 0], jnp.int32) // KBLOCK
            give, given = conv_rows(other + ahead, source, g_parts, step, whole, after)
            taken.append(lax.ppermute(give, "tm", pairs(slabs, 1)))
            after = (given,)
        keep, kept = conv_rows(own, source, g_parts, part, whole, after)
        mine = keep + (jnp.concatenate(taken, axis=0) if len(taken) > 1 else taken[0])
        before = (kept, mark_of(mine))
        bit = 2
        while 2 * bit < slabs:
            mine = mine + lax.ppermute(mine, "tm", pairs(slabs, bit))
            bit *= 2
        return (mine, lax.ppermute(mine, "tm", pairs(slabs, bit))), before

    def summed(two, after=()):
        mine, mark = added(*two, after) if after else (two[0] + two[1], None)
        return (mine, lax.ppermute(mine, "tm", pairs(slabs, 1))), (mark_of(mine) if mark is None else mark,)

    def updated(conv, g_parts, chunk, cuts, after=()):
        out = ()
        for j, halves in enumerate(conv):
            *out, mark = update_rows(
                infos_of[len(conv)][j][0], halves, panel_start, g_parts, chunk, count, step_scale, cuts, out, after
            )
            after = ()
        return out, (mark,)

    sent = [cut_rows(panel_start, c, total, count) for c in range(CHUNKS)]
    tables = table_parts(ordering)
    guess = gathered(block_guess)
    g_parts = [panel_start]
    before = tuple(mark_of(x) for x in guess)
    for sweep in range(PASSES):
        last = sweep == PASSES - 1
        arrived = [exchange(x) for x in sent]
        sigma = []
        for chunk in range(CHUNKS):
            site = arrived[chunk].reshape(K, spins, rows, LANES)
            cuts = PIECES if last and chunk == CHUNKS - 1 else 1
            *parts, mark = site_sigma(strength, weights, tables, site, count, cuts, before)
            before = (mark,)
            sigma.append([exchange(x.reshape(count, -1, spins, rows, LANES)) for x in parts])
        pending, news = [], []
        for chunk in range(CHUNKS - 1 if last else CHUNKS):
            pieces = 1 if last else PIECES
            twos = []
            for j in range(pieces):
                two, before = convolved(sigma[chunk], g_parts, pieces, j, before)
                twos.append(two)
            if last:
                pending.append(twos)
            else:
                sums = [summed(two) for two in twos]
                before = tuple(mark for _, marks in sums for mark in marks)
                new, before = updated([conv for conv, _ in sums], g_parts, chunk, True, before)
                news.append(new)
        if not last:
            g_parts = [n[0] for n in news]
            sent = [n[1] for n in news]

    def final_piece(j, conv, out, after):
        for which in range(2):
            *out, mark = final_rows(
                infos_of[PIECES][j][which], j, past, conv[which], panel_start, nows, g_parts, guess, step_scale, out, after
            )
            after = ()
        return out, (mark,)

    out, nows, past = (), [], []
    for j in range(PIECES):
        two, beside = convolved(sigma[-1], g_parts, PIECES, j, before)
        if j == 0:
            for c, twos in enumerate(pending):
                sums = [summed(two) for two in twos]
                new, beside = updated([conv for conv, _ in sums], g_parts, c, False, beside)
                nows.append(new[0])
                past.append(sums[0][0])
        else:
            out, beside = final_piece(j - 1, conv, out, beside)
        conv, before = summed(two, beside)
    return final_piece(PIECES - 1, conv, out, ())[0][0]


def fits(mesh):
    def tiled(panel_start, *_):
        momenta, spins, panel, width = panel_start.shape
        count, slabs = mesh.shape["mom"], mesh.shape["tm"]
        powers = all(n & (n - 1) == 0 for n in (count, slabs))
        local = momenta // count
        return (
            powers
            and slabs > 2
            and spins == 2 * mesh.shape["groups"]
            and width == LANES * slabs
            and 2 * panel == LANES
            and panel == CHUNKS * count * ROWS
            and local % (2 * PIECES * WIDE * KBLOCK) == 0
            and PIECES == 2
            and PASSES == 2
        )

    return tiled


def solution(mesh):
    def mapped(inner):
        return jax.shard_map(
            inner,
            mesh=mesh,
            in_specs=(
                P("mom", "groups", None, "tm"),
                P("mom", "groups", "tm", None),
                P("groups"),
                P("groups"),
                P("groups"),
                P(),
            ),
            out_specs=P("mom", "groups", None, "tm"),
            check_vma=False,
        )

    def chosen(*args):
        return mapped(body if fits(mesh)(*args) else plain_body)(*args)

    return chosen
```
